256 devices in a mesh: dp: 16 (over z, core), seq: 16 (over x, y).
Axes of the slice: x: 4, y: 4, z: 8, core: 2. Of those that a mesh axis runs over, the one named last changes fastest.
Arguments:
- queries: bfloat16 [16, 2048, 2048], P('dp', 'seq'), may hold values from -30 to 30
- keys_in: bfloat16 [16, 2048, 2048], P('dp', 'seq'), may hold values from -30 to 30
- values_in: bfloat16 [16, 2048, 2048], P('dp', 'seq'), may hold values from -1.5 to 1.5
- saved_out: bfloat16 [16, 2048, 2048], P('dp', 'seq'), may hold values from -0.75 to 0.75
- out_grad: bfloat16 [16, 2048, 3200], P('dp', 'seq'), may hold values from -6 to 6
- out_weight: bfloat16 [2048, 3200], P('seq'), may hold values from -0.125 to 0.125
- image_units: int32 [16, 8], P('dp'), may hold values from 1 to 32, 128 in all within a row
Outputs:
- query_grad: bfloat16 [16, 2048, 2048], P('dp', 'seq')
- key_grad: bfloat16 [16, 2048, 2048], P('dp', 'seq')
- value_grad: bfloat16 [16, 2048, 2048], P('dp', 'seq')
- weight_grad: float32 [2048, 3200], P('seq', 'dp')
The draws below stay inside these ranges and needn't reach their ends.
Inputs may be any that keep to these rules, and one draw needn't show every extreme that they name: `image_units`: each row sums to 128 and its largest entry is 32.
All inputs are finite; a program needn't handle non-finite values.
Results may differ from the reference program's by a relative error of at most 0.015.
Values may be sent and summed in bfloat16 or wider, within the bound.
No kernel may reach another device: no remote copies, remote signals or barrier semaphores. Data moves between devices by JAX's collectives and lax.ppermute only.
A program may use at most 128 MiB of HBM per device.

```python
import math
import jax
import jax.numpy as jnp
import numpy as np
from jax import lax

D = 3200
HEADS = 16
HEAD_DIM = 128
TOK_DEV = 128
PACK = 2048
IMG_MAX = 512
PACKS = 16
SEGS = 8
N_SEQ = 16


def draw_queries(key, part):
    key = jax.random.fold_in(key, 11)
    shape = (PACKS, PACK, HEADS * HEAD_DIM)
    return jnp.clip(jax.random.normal(key, shape, jnp.float32), -6.0, 6.0).astype(jnp.bfloat16)


def draw_keys_in(key, part):
    key = jax.random.fold_in(key, 23)
    shape = (PACKS, PACK, HEADS * HEAD_DIM)
    return jnp.clip(jax.random.normal(key, shape, jnp.float32), -6.0, 6.0).astype(jnp.bfloat16)


def strengthened(values, stream_key, source, target, shards_of, factor):
    def block_of(position):
        return (jnp.arange(values.shape[position]) // (values.shape[position] // shards_of)).reshape((-1,) + (1,) * (values.ndim - 1 - position))

    one_side = jax.random.permutation(stream_key, shards_of)[block_of(target)]
    other_side = (block_of(target) + shards_of // 2) % shards_of
    return jnp.where((block_of(source) == one_side) | (block_of(source) == other_side), factor * values, values)


def level_of(rng, extent, cuts, smallest, high):
    def one(axis_at, blocks):
        draws = jax.random.uniform(jax.random.fold_in(jax.random.fold_in(rng, 6), axis_at), (blocks,), jnp.float32, smallest / len(cuts), high / len(cuts))
        return jnp.repeat(jnp.exp(draws), extent[axis_at] // blocks).reshape((-1,) + (1,) * (len(extent) - axis_at - 1))

    factor_of = one(*cuts[0])
    for cut in cuts[1:]:
        factor_of = factor_of * one(*cut)
    return factor_of


def profile(number_of, total, limit, slope):
    weights = [(1 << 20) // math.isqrt(rank ** slope) + 1 for rank in range(2, number_of + 1)]
    spare, counts = total - limit - (number_of - 1), [1] * (number_of - 1)
    while spare > 0:
        candidates = [i for i in range(number_of - 1) if counts[i] < limit]
        pool, budget = sum([weights[i] for i in candidates]), spare
        for i in candidates:
            addition = min(limit - counts[i], max(1, budget * weights[i] // pool), spare)
            counts[i] = counts[i] + addition
            spare = spare - addition
    return np.array([limit] + counts)


def uneven_parts(key, number_of, total, most, skew):
    if number_of == 2:
        one = jax.random.randint(key, (), max(1, total - most), min(most, total - 1) + 1)
        return jnp.stack([one, total - one])
    tallies = jnp.asarray(profile(number_of, total, most, skew), jnp.int32)
    pairs = (number_of - 1) // 2
    giver, receiver = tallies[1:1 + 2 * pairs:2], tallies[2:2 + 2 * pairs:2]
    slack = jnp.minimum(giver - 1, most - receiver)
    shifted = jax.random.randint(jax.random.fold_in(key, 1), (pairs,), 0, 1 << 20) % (slack + 1)
    tallies = tallies.at[1:1 + 2 * pairs:2].set(giver - shifted).at[2:2 + 2 * pairs:2].set(receiver + shifted)
    return tallies[jax.random.permutation(jax.random.fold_in(key, 2), number_of)]


def noise(stream_key, dims, spread, most, shards=(), held_as=jnp.bfloat16):
    level = level_of(stream_key, dims, shards, -0.22, 0.18) if shards else 1.0
    result = jax.random.normal(stream_key, dims, jnp.float32) * spread * level
    return jnp.minimum(jnp.maximum(result, -most), most).astype(held_as)


def bell_draw_with(own_key, shape, scale, most, cuts, heavy, held_as=jnp.bfloat16):
    drawn = scale * jax.random.normal(own_key, shape, jnp.float32)
    if cuts:
        drawn = drawn * level_of(own_key, shape, cuts, -0.22, 0.18)
    return jnp.clip(strengthened(drawn, jax.random.fold_in(own_key, 3), *heavy), -most, most).astype(held_as)


def setup_inputs(seed: int = 0) -> dict:
    key_of = jax.random.split(jax.random.key(seed), 8)
    return {
        "queries": draw_queries(jax.random.fold_in(key_of[7], 71), 0),
        "keys_in": draw_keys_in(jax.random.fold_in(key_of[7], 71), 0),
        "values_in": noise(key_of[2], (PACKS, PACK, HEADS * HEAD_DIM), 0.25, 1.5, ((0, 16), (1, 16))),
        "saved_out": bell_draw_with(key_of[3], (PACKS, PACK, HEADS * HEAD_DIM), 0.125, 0.75, ((0, 16), (1, 16)), (1, 2, 16, 2.0)),
        "out_grad": bell_draw_with(key_of[4], (PACKS, PACK, D), 1.0, 6.0, ((0, 16), (1, 16)), (0, 2, 16, 2.0)),
        "out_weight": noise(key_of[5], (HEADS * HEAD_DIM, D), (HEADS * HEAD_DIM) ** -0.5, 0.125, ((0, 16),)),
        "image_units": jax.vmap(lambda own: uneven_parts(own, SEGS, PACK // 16, IMG_MAX // 16, 2))(jax.random.split(key_of[6], PACKS)).reshape((PACKS, SEGS)).astype(jnp.int32),
    }


def image_tables(units, length):
    sizes = (units * 16).astype(jnp.int32)
    bounds = jnp.cumsum(sizes).astype(jnp.int32)
    places = jnp.arange(length, dtype=jnp.int32)
    owners = lax.optimization_barrier(jnp.sum((places[:, None] >= bounds[None, :]).astype(jnp.int32), axis=1)).astype(jnp.int32)
    openings = lax.optimization_barrier(jnp.sum(jnp.where(bounds[None, :] <= places[:, None], sizes[None, :], 0), axis=1)).astype(jnp.int32)
    return (owners, openings)

def as_float(value):
    return value.astype(jnp.float32)

def attend_back(query_head, key_head, value_head, output_head, grad_head, owners, openings, key_span):
    length, columns = query_head.shape
    head_count = columns // HEAD_DIM
    block_rows = min(length, 512)
    scaling = 1.0 / math.sqrt(HEAD_DIM)
    split_shape = (length, head_count, HEAD_DIM)
    query_split = query_head.reshape(split_shape)
    key_split = key_head.reshape(split_shape)
    value_split = value_head.reshape(split_shape)
    output_split = output_head.reshape(split_shape)
    grad_split = grad_head.reshape(split_shape)

    def one_block(counter, running):
        query_acc, key_acc, value_acc = running
        first_row = (counter * block_rows).astype(jnp.int32)
        key_start = jnp.minimum(lax.dynamic_index_in_dim(openings, first_row, keepdims=False), length - key_span).astype(jnp.int32)
        query_rows = lax.dynamic_slice_in_dim(query_split, first_row, block_rows, 0)
        key_rows = lax.dynamic_slice_in_dim(key_split, key_start, key_span, 0)
        value_rows = lax.dynamic_slice_in_dim(value_split, key_start, key_span, 0)
        out_rows = lax.dynamic_slice_in_dim(output_split, first_row, block_rows, 0)
        grad_rows = lax.dynamic_slice_in_dim(grad_split, first_row, block_rows, 0)
        same_image = lax.dynamic_slice_in_dim(owners, first_row, block_rows, 0)[:, None] == lax.dynamic_slice_in_dim(owners, key_start, key_span, 0)[None, :]
        scores = jnp.einsum('qhd,khd->hqk', as_float(query_rows), as_float(key_rows)) * scaling
        scores = jnp.where(same_image[None], scores, jnp.float32(-1e+30))
        largest = lax.optimization_barrier(jnp.max(scores, axis=2, keepdims=True))
        log_total = largest + jnp.log(lax.optimization_barrier(jnp.sum(jnp.exp(scores - largest), axis=2, keepdims=True)))
        weights = jnp.exp(scores - log_total)
        weights_low = weights.astype(jnp.bfloat16)
        row_delta = lax.optimization_barrier(jnp.sum(as_float(grad_rows) * as_float(out_rows), axis=2)).T
        weight_grads = jnp.einsum('qhd,khd->hqk', as_float(grad_rows), as_float(value_rows))
        score_grads = (weights * (weight_grads - row_delta[:, :, None])).astype(jnp.bfloat16)
        query_part = jnp.einsum('hqk,khd->qhd', as_float(score_grads), as_float(key_rows)) * scaling
        key_part = jnp.einsum('hqk,qhd->khd', as_float(score_grads), as_float(query_rows)) * scaling
        value_part = jnp.einsum('hqk,qhd->khd', as_float(weights_low), as_float(grad_rows))
        query_acc = lax.dynamic_update_slice_in_dim(query_acc, query_part, first_row, 0)
        key_acc = lax.dynamic_update_slice_in_dim(key_acc, lax.dynamic_slice_in_dim(key_acc, key_start, key_span, 0) + key_part, key_start, 0)
        value_acc = lax.dynamic_update_slice_in_dim(value_acc, lax.dynamic_slice_in_dim(value_acc, key_start, key_span, 0) + value_part, key_start, 0)
        return (query_acc, key_acc, value_acc)
    empty_acc = jnp.zeros(split_shape, jnp.float32)
    results = lax.fori_loop(0, length // block_rows, one_block, (empty_acc, empty_acc, empty_acc))
    return tuple((item.reshape(length, columns).astype(jnp.bfloat16) for item in results))

def reference(queries, keys_in, values_in, saved_out, out_grad, out_weight, image_units):
    key_span = min(PACK, min(PACK, 512) + 2 * IMG_MAX)

    def one_pack(items):
        query_head, key_head, value_head, output_head, grad_pack, units = items
        owners, openings = image_tables(units, PACK)
        head_grad = jnp.dot(grad_pack, out_weight.T, preferred_element_type=jnp.float32).astype(jnp.bfloat16)
        return attend_back(query_head, key_head, value_head, output_head, head_grad, owners, openings, key_span)
    query_grad, key_grad, value_grad = lax.map(one_pack, (queries, keys_in, values_in, saved_out, out_grad, image_units))
    outs_split = saved_out.reshape(PACKS * N_SEQ, TOK_DEV, HEADS * HEAD_DIM)
    grads_split = out_grad.reshape(PACKS * N_SEQ, TOK_DEV, D)

    def add_shard(summed, shard_pair):
        term = jnp.dot(shard_pair[0].T, shard_pair[1], preferred_element_type=jnp.float32)
        term = lax.optimization_barrier(term.astype(jnp.bfloat16)).astype(jnp.float32)
        return (summed + term, None)
    summed = lax.scan(add_shard, jnp.zeros((HEADS * HEAD_DIM, D), jnp.float32), (outs_split, grads_split))[0]
    weight_grad = summed * (1.0 / math.sqrt(PACKS * PACK))
    return (query_grad, key_grad, value_grad, weight_grad)
```

```python
import math

import jax
import jax.numpy as jnp
from jax import lax
from jax.experimental import pallas as pl
from jax.experimental.pallas import tpu as pltpu
from jax.sharding import PartitionSpec as P

HEAD = 128
PACK = 2048
TOK = 128
MODEL = 3200
IMG = 512
SEGS = 8
NEG = -1e30
BF = jnp.bfloat16
F32 = jnp.float32
XS = [[(4 * x + y, 4 * ((x + k) % 4) + y) for x in range(4) for y in range(4)] for k in range(4)]
YS = [[(4 * x + y, 4 * x + (y + k) % 4) for x in range(4) for y in range(4)] for k in range(4)]
YGROUPS = [[4 * x + y for y in range(4)] for x in range(4)]
CORES = [(i, i ^ 1) for i in range(16)]
ZGROUPS = [[2 * z + c for z in range(8)] for c in range(2)]


def nt(a, b):
    return lax.dot_general(a, b, (((1,), (1,)), ((), ())), preferred_element_type=F32)


def nn(a, b):
    return lax.dot_general(a, b, (((1,), (0,)), ((), ())), preferred_element_type=F32)


def tn(a, b):
    return lax.dot_general(a, b, (((0,), (0,)), ((), ())), preferred_element_type=F32)


def attention_kernel(xi, units, qkv, h0, h1, h2, h3, out, qs, ks, vs, hs, ds_, gq, gk, gv):
    for i in range(16):
        rows = pl.ds(i * TOK, TOK)
        qs[rows, :] = qkv[i, 0]
        ks[rows, :] = qkv[i, 1]
        vs[rows, :] = qkv[i, 2]
    tail = pl.ds(PACK, IMG)
    for ref in (qs, ks, vs, hs):
        ref[tail, :] = jnp.zeros((IMG, HEAD), BF)
    ds_[pl.ds(16, 8), :] = jnp.zeros((8, HEAD), F32)
    for k, h in enumerate((h0, h1, h2, h3)):
        block = lax.rem(xi[0] + k, 4)
        hs[pl.ds(pl.multiple_of(block * IMG, IMG), IMG), :] = h[pl.ds(0, IMG), :]
        parts = h[pl.ds(IMG, 16), :].astype(F32)
        ds_[pl.ds(block * 4, 4), :] = parts[0:4] + parts[4:8] + parts[8:12]
    scaling = 1.0 / math.sqrt(HEAD)
    to_two = scaling * math.log2(math.e)

    def image(start, size, width, step):
        kw = ks[pl.ds(start, width), :]
        vw = vs[pl.ds(start, width), :]
        row = lax.broadcasted_iota(jnp.int32, (width, 1), 0)
        bias = jnp.where(row < size, 0.0, NEG).astype(F32)
        first = lax.div(start, TOK)
        shift = start - first * TOK
        gk_sum = gv_sum = None
        for b in range(width // step):
            here = pl.ds(pl.multiple_of(start + b * step, 16), step)
            qb = qs[here, :]
            hb = hs[here, :]
            lane = lax.broadcasted_iota(jnp.int32, (1, step), 1) + b * step
            pieces = []
            for n in range(step // TOK):
                line = first + b * (step // TOK) + n
                two = jnp.concatenate([ds_[pl.ds(line, 1), :], ds_[pl.ds(line + 1, 1), :]], axis=1)
                pieces.append(pltpu.roll(two, 2 * TOK - shift, 1)[:, :TOK])
            delta = pieces[0] if len(pieces) == 1 else jnp.concatenate(pieces, axis=1)
            s = nt(kw, qb) * to_two + bias
            top = jnp.max(s, axis=0, keepdims=True)
            e = jnp.exp2(s - top)
            norm = jnp.where(lane < size, 1.0 / jnp.sum(e, axis=0, keepdims=True), 0.0)
            p = e * norm
            dp = nt(vw, hb)
            dsc = (p * (dp - delta)).astype(BF)
            pk = nn(dsc, qb)
            pv = nn(p.astype(BF), hb)
            gk_sum = pk if gk_sum is None else gk_sum + pk
            gv_sum = pv if gv_sum is None else gv_sum + pv
            gq[here, :] = (tn(dsc, kw) * scaling).astype(BF)
        gk[pl.ds(start, width), :] = (gk_sum * scaling).astype(BF)
        gv[pl.ds(start, width), :] = gv_sum.astype(BF)

    def one(j, start):
        size = units[j] * 16
        start = pl.multiple_of(start, 16)
        for width, step in ((128, 128), (256, 256), (384, 384), (512, 256)):
            pl.when((size > width - 128) & (size <= width))(lambda width=width, step=step: image(start, size, width, step))
        return start + size

    lax.fori_loop(0, SEGS, one, jnp.int32(0))
    for i in range(16):
        rows = pl.ds(i * TOK, TOK)
        out[i, 0] = gq[rows, :]
        out[i, 1] = gk[rows, :]
        out[i, 2] = gv[rows, :]


def attention(xi, units, qkv, hs):
    vm = pl.BlockSpec(memory_space=pltpu.VMEM)
    sm = pl.BlockSpec(memory_space=pltpu.SMEM)
    return pl.pallas_call(
        attention_kernel,
        out_shape=jax.ShapeDtypeStruct((16, 3, TOK, HEAD), BF),
        in_specs=[sm, sm] + [vm] * 5,
        out_specs=vm,
        scratch_shapes=[pltpu.VMEM((PACK + IMG, HEAD), BF)] * 4 + [pltpu.VMEM((24, HEAD), F32)] + [pltpu.VMEM((PACK + IMG, HEAD), BF)] * 3,
        compiler_params=pltpu.CompilerParams(vmem_limit_bytes=40 * 1024 * 1024),
        cost_estimate=pl.CostEstimate(flops=2 * 5 * 128 * 900000, bytes_accessed=4 * 1024 * 1024, transcendentals=900000),
        name="attention",
    )(xi, units, qkv, *hs)


def pack_kernel(q, k, v, out):
    for i in range(16):
        cols = pl.ds(i * HEAD, HEAD)
        out[i, 0] = q[:, cols]
        out[i, 1] = k[:, cols]
        out[i, 2] = v[:, cols]


def pack(q, k, v):
    vm = pl.BlockSpec(memory_space=pltpu.VMEM)
    return pl.pallas_call(
        pack_kernel,
        out_shape=jax.ShapeDtypeStruct((16, 3, TOK, HEAD), BF),
        in_specs=[vm] * 3,
        out_specs=vm,
        cost_estimate=pl.CostEstimate(flops=0, bytes_accessed=3 * 1024 * 1024, transcendentals=0),
        name="pack",
    )(q, k, v)


def unpack_kernel(grads, q, k, v):
    for i in range(16):
        cols = pl.ds(i * HEAD, HEAD)
        q[:, cols] = grads[i, 0]
        k[:, cols] = grads[i, 1]
        v[:, cols] = grads[i, 2]


def unpack(grads):
    vm = pl.BlockSpec(memory_space=pltpu.VMEM)
    return pl.pallas_call(
        unpack_kernel,
        out_shape=[jax.ShapeDtypeStruct((TOK, 16 * HEAD), BF)] * 3,
        in_specs=[vm],
        out_specs=[vm] * 3,
        cost_estimate=pl.CostEstimate(flops=0, bytes_accessed=3 * 1024 * 1024, transcendentals=0),
        name="unpack",
    )(grads)


def three_terms(value):
    high = value.astype(BF)
    rest = value - high.astype(F32)
    middle = rest.astype(BF)
    return jnp.concatenate([high, middle, (rest - middle.astype(F32)).astype(BF), jnp.zeros_like(high)], axis=0)


def on_device(queries, keys_in, values_in, saved_out, out_grad, out_weight, image_units):
    seq = lax.axis_index("seq")
    dp = lax.axis_index("dp")
    x, y, core = seq // 4, seq % 4, dp % 2
    g = out_grad[0]

    o_sent = saved_out[0].reshape(TOK, 4, 4, HEAD).transpose(2, 0, 1, 3).reshape(4, TOK, 4 * HEAD)
    o_rows = lax.all_to_all(o_sent, "seq", split_axis=0, concat_axis=0, tiled=True, axis_index_groups=YGROUPS)

    g_back = lax.ppermute(g, "seq", YS[1])
    g_next = lax.ppermute(g, "seq", YS[3])
    w_parts = [out_weight] + [lax.ppermute(out_weight, "seq", XS[k]) for k in (1, 2, 3)]
    g_far = jnp.concatenate([lax.ppermute(g_back[:64], "seq", YS[1]), lax.ppermute(g_next[64:], "seq", YS[3])], axis=0)
    g_rows = lax.dynamic_slice_in_dim(
        jnp.concatenate([g, g_next, g_far, g_back, g, g_next, g_far], axis=0), lax.rem(4 - y, 4) * TOK, 4 * TOK, 0
    )
    w_rows = jnp.concatenate(w_parts, axis=0)
    head = nt(g_rows, w_rows).astype(BF)
    o_flat = o_rows.reshape(4 * TOK, 4, HEAD)

    h_parts = []
    for k in range(4):
        hk = head[:, k * HEAD : (k + 1) * HEAD]
        ok = lax.dynamic_index_in_dim(o_flat, lax.rem(x + 4 - k, 4), 1, keepdims=False)
        delta = jnp.sum(hk.astype(F32) * ok.astype(F32), axis=1).reshape(4, TOK)
        hk = jnp.concatenate([hk, three_terms(delta)], axis=0)
        h_parts.append(lax.ppermute(hk, "seq", XS[4 - k]) if k else hk)

    qkv = lax.all_to_all(
        pack(queries[0], keys_in[0], values_in[0]), "seq", split_axis=0, concat_axis=0, tiled=True
    )
    grads = attention(x.astype(jnp.int32)[None], image_units[0], qkv, h_parts)
    back = lax.all_to_all(grads, "seq", split_axis=0, concat_axis=0, tiled=True)
    query_grad, key_grad, value_grad = unpack(back)

    term = tn(g_rows, o_rows.reshape(4 * TOK, 4 * HEAD)).astype(BF).reshape(8, 2, 200, 4 * HEAD)
    mine = lax.dynamic_index_in_dim(term, core, 1, keepdims=False)
    other = lax.ppermute(lax.dynamic_index_in_dim(term, 1 - core, 1, keepdims=False), "dp", CORES)
    both = (mine.astype(F32) + other.astype(F32)).astype(BF).reshape(1600, 4 * HEAD)
    summed = lax.psum_scatter(both, "dp", scatter_dimension=0, tiled=True, axis_index_groups=ZGROUPS)
    blocks = summed.astype(F32).reshape(200, 4, HEAD)
    weight = lax.dynamic_index_in_dim(blocks, x, 1, keepdims=False)
    for k in (1, 2, 3):
        weight = weight + lax.ppermute(
            lax.dynamic_index_in_dim(blocks, lax.rem(x + k, 4), 1, keepdims=False), "seq", XS[k]
        )
    weight_grad = weight.T * (1.0 / math.sqrt(PACK * 16))
    return query_grad[None], key_grad[None], value_grad[None], weight_grad


def solution(mesh):
    rows = P("dp", "seq", None)
    return jax.shard_map(
        on_device,
        mesh=mesh,
        in_specs=(rows, rows, rows, rows, rows, P("seq", None), P("dp", None)),
        out_specs=(rows, rows, rows, P("seq", "dp")),
        check_vma=False,
    )
```

```python
import math

import jax
import jax.numpy as jnp
from jax import lax
from jax.experimental import pallas as pl
from jax.experimental.pallas import tpu as pltpu
from jax.sharding import PartitionSpec as P

HEAD = 128
PACK = 2048
TOK = 128
MODEL = 3200
IMG = 512
SEGS = 8
NEG = -1e30
BF = jnp.bfloat16
F32 = jnp.float32
XS = [[(4 * x + y, 4 * ((x + k) % 4) + y) for x in range(4) for y in range(4)] for k in range(4)]
YS = [[(4 * x + y, 4 * x + (y + k) % 4) for x in range(4) for y in range(4)] for k in range(4)]
YGROUPS = [[4 * x + y for y in range(4)] for x in range(4)]
CORES = [(i, i ^ 1) for i in range(16)]
ZS = [[(2 * z + c, 2 * (z ^ b) + c) for z in range(8) for c in range(2)] for b in (1, 2, 4)]
BOTH = [
    (16 * d + 4 * x + y, 16 * d + 4 * ((x + (1, 3)[d % 2]) % 4) + y)
    for d in range(16)
    for x in range(4)
    for y in range(4)
]
CHUNK = 640


def nt(a, b):
    return lax.dot_general(a, b, (((1,), (1,)), ((), ())), preferred_element_type=F32)


def nn(a, b):
    return lax.dot_general(a, b, (((1,), (0,)), ((), ())), preferred_element_type=F32)


def tn(a, b):
    return lax.dot_general(a, b, (((0,), (0,)), ((), ())), preferred_element_type=F32)


def attention_kernel(xi, units, qkv, h0, h1, h2, h3, out, qs, ks, vs, hs, ds_, gq, gk, gv):
    for i in range(16):
        rows = pl.ds(i * TOK, TOK)
        qs[rows, :] = qkv[i, 0]
        ks[rows, :] = qkv[i, 1]
        vs[rows, :] = qkv[i, 2]
    tail = pl.ds(PACK, IMG)
    for ref in (qs, ks, vs, hs):
        ref[tail, :] = jnp.zeros((IMG, HEAD), BF)
    ds_[pl.ds(16, 8), :] = jnp.zeros((8, HEAD), F32)
    for k, h in enumerate((h0, h1, h2, h3)):
        block = lax.rem(xi[0] + k, 4)
        hs[pl.ds(pl.multiple_of(block * IMG, IMG), IMG), :] = h[pl.ds(0, IMG), :]
        parts = h[pl.ds(IMG, 16), :].astype(F32)
        ds_[pl.ds(block * 4, 4), :] = parts[0:4] + parts[4:8] + parts[8:12]
    scaling = 1.0 / math.sqrt(HEAD)
    to_two = scaling * math.log2(math.e)

    def image(start, size, width, step):
        kw = ks[pl.ds(start, width), :]
        vw = vs[pl.ds(start, width), :]
        row = lax.broadcasted_iota(jnp.int32, (width, 1), 0)
        bias = jnp.where(row < size, 0.0, NEG).astype(F32)
        first = lax.div(start, TOK)
        shift = start - first * TOK
        gk_sum = gv_sum = None
        for b in range(width // step):
            here = pl.ds(pl.multiple_of(start + b * step, 16), step)
            qb = qs[here, :]
            hb = hs[here, :]
            lane = lax.broadcasted_iota(jnp.int32, (1, step), 1) + b * step
            pieces = []
            for n in range(step // TOK):
                line = first + b * (step // TOK) + n
                two = jnp.concatenate([ds_[pl.ds(line, 1), :], ds_[pl.ds(line + 1, 1), :]], axis=1)
                pieces.append(pltpu.roll(two, 2 * TOK - shift, 1)[:, :TOK])
            delta = pieces[0] if len(pieces) == 1 else jnp.concatenate(pieces, axis=1)
            s = nt(kw, qb) * to_two + bias
            top = jnp.max(s, axis=0, keepdims=True)
            e = jnp.exp2(s - top)
            norm = jnp.where(lane < size, 1.0 / jnp.sum(e, axis=0, keepdims=True), 0.0)
            p = e * norm
            dp = nt(vw, hb)
            dsc = (p * (dp - delta)).astype(BF)
            pk = nn(dsc, qb)
            pv = nn(p.astype(BF), hb)
            gk_sum = pk if gk_sum is None else gk_sum + pk
            gv_sum = pv if gv_sum is None else gv_sum + pv
            gq[here, :] = (tn(dsc, kw) * scaling).astype(BF)
        gk[pl.ds(start, width), :] = (gk_sum * scaling).astype(BF)
        gv[pl.ds(start, width), :] = gv_sum.astype(BF)

    def one(j, start):
        size = units[j] * 16
        start = pl.multiple_of(start, 16)
        for width, step in ((128, 128), (256, 256), (384, 384), (512, 256)):
            pl.when((size > width - 128) & (size <= width))(lambda width=width, step=step: image(start, size, width, step))
        return start + size

    lax.fori_loop(0, SEGS, one, jnp.int32(0))
    for i in range(16):
        rows = pl.ds(i * TOK, TOK)
        out[i, 0] = gq[rows, :]
        out[i, 1] = gk[rows, :]
        out[i, 2] = gv[rows, :]


def attention(xi, units, qkv, hs):
    vm = pl.BlockSpec(memory_space=pltpu.VMEM)
    sm = pl.BlockSpec(memory_space=pltpu.SMEM)
    return pl.pallas_call(
        attention_kernel,
        out_shape=jax.ShapeDtypeStruct((16, 3, TOK, HEAD), BF),
        in_specs=[sm, sm] + [vm] * 5,
        out_specs=vm,
        scratch_shapes=[pltpu.VMEM((PACK + IMG, HEAD), BF)] * 4 + [pltpu.VMEM((24, HEAD), F32)] + [pltpu.VMEM((PACK + IMG, HEAD), BF)] * 3,
        compiler_params=pltpu.CompilerParams(vmem_limit_bytes=40 * 1024 * 1024),
        cost_estimate=pl.CostEstimate(flops=10350000000, bytes_accessed=32400000, transcendentals=0),
        name="attention",
    )(xi, units, qkv, *hs)


def pack_kernel(q, k, v, out):
    for i in range(16):
        cols = pl.ds(i * HEAD, HEAD)
        out[i, 0] = q[:, cols]
        out[i, 1] = k[:, cols]
        out[i, 2] = v[:, cols]


def pack(q, k, v):
    vm = pl.BlockSpec(memory_space=pltpu.VMEM)
    return pl.pallas_call(
        pack_kernel,
        out_shape=jax.ShapeDtypeStruct((16, 3, TOK, HEAD), BF),
        in_specs=[vm] * 3,
        out_specs=vm,
        cost_estimate=pl.CostEstimate(flops=1, bytes_accessed=1, transcendentals=0),
        name="pack",
    )(q, k, v)


def unpack_kernel(grads, q, k, v):
    for i in range(16):
        cols = pl.ds(i * HEAD, HEAD)
        q[:, cols] = grads[i, 0]
        k[:, cols] = grads[i, 1]
        v[:, cols] = grads[i, 2]


def unpack(grads):
    vm = pl.BlockSpec(memory_space=pltpu.VMEM)
    return pl.pallas_call(
        unpack_kernel,
        out_shape=[jax.ShapeDtypeStruct((TOK, 16 * HEAD), BF)] * 3,
        in_specs=[vm],
        out_specs=[vm] * 3,
        cost_estimate=pl.CostEstimate(flops=1, bytes_accessed=1, transcendentals=0),
        name="unpack",
    )(grads)


def three_terms(value):
    high = value.astype(BF)
    rest = value - high.astype(F32)
    middle = rest.astype(BF)
    return jnp.concatenate([high, middle, (rest - middle.astype(F32)).astype(BF), jnp.zeros_like(high)], axis=0)


def pack_out_kernel(o, out):
    for y in range(4):
        for x in range(4):
            out[y, :, pl.ds(x * HEAD, HEAD)] = o[:, pl.ds((4 * x + y) * HEAD, HEAD)]


def pack_out(o):
    vm = pl.BlockSpec(memory_space=pltpu.VMEM)
    return pl.pallas_call(
        pack_out_kernel,
        out_shape=jax.ShapeDtypeStruct((4, TOK, 4 * HEAD), BF),
        in_specs=[vm],
        out_specs=vm,
        cost_estimate=pl.CostEstimate(flops=1, bytes_accessed=1, transcendentals=0),
        name="pack_out",
    )(o)


def chunk_copies(pieces, whole, sems, c):
    cols = pl.ds(c * CHUNK, CHUNK)
    copies = []
    for n, (ref, row) in enumerate(pieces):
        rows = ref.shape[0]
        copies.append(
            pltpu.make_async_copy(
                ref.at[:, cols], whole.at[pl.ds(pl.multiple_of(row, 64), rows), cols], sems.at[c, n]
            )
        )
    return copies


def grad_pieces(y, g, back, ahead, fa, fb):
    far = lax.rem(y + 2, 4) * TOK
    return [(g, y * TOK), (back, lax.rem(y + 3, 4) * TOK), (ahead, lax.rem(y + 1, 4) * TOK), (fa, far), (fb, far + 64)]


def head_kernel(at, *refs):
    g, (w, wa, wb, wc, wd, o), hs, (gs, ws, acc, gsem, wsem) = refs[:5], refs[5:11], refs[11:15], refs[15:]
    x, y, core = at[0], at[1], at[2]
    g_pieces = grad_pieces(y, *g)
    near = lax.select(core == 0, 1, 3)
    w_pieces = [
        (w, 0),
        (wa, near * TOK),
        (wb, (4 - near) * TOK),
        (wc, 2 * TOK + 64 * core),
        (wd, 2 * TOK + 64 * (1 - core)),
    ]
    copies = [chunk_copies(w_pieces, ws, wsem, c) + chunk_copies(g_pieces, gs, gsem, c) for c in range(MODEL // CHUNK)]
    for group in copies:
        for copy in group:
            copy.start()
    for c, group in enumerate(copies):
        for copy in group:
            copy.wait()
        cols = pl.ds(c * CHUNK, CHUNK)
        part = nt(gs[:, cols], ws[:, cols])
        if c == 0:
            acc[...] = part
        else:
            acc[...] += part
    for k in range(4):
        own = pl.ds(pl.multiple_of(lax.rem(x + 4 - k, 4) * HEAD, HEAD), HEAD)
        lines = []
        for j in range(4):
            rows = pl.ds(j * TOK, TOK)
            h = acc[rows, pl.ds(k * HEAD, HEAD)].astype(BF)
            hs[k][rows, :] = h
            product = h.astype(F32) * o[j, :, own].astype(F32)
            lines.append(jnp.sum(product.T, axis=0, keepdims=True))
        hs[k][pl.ds(4 * TOK, 16), :] = three_terms(jnp.concatenate(lines, axis=0))


def head_blocks(at, g, w, o):
    vm = pl.BlockSpec(memory_space=pltpu.VMEM)
    sm = pl.BlockSpec(memory_space=pltpu.SMEM)
    hbm = pl.BlockSpec(memory_space=pl.ANY)
    return pl.pallas_call(
        head_kernel,
        out_shape=[jax.ShapeDtypeStruct((4 * TOK + 16, HEAD), BF)] * 4,
        in_specs=[sm] + [hbm] * 10 + [vm],
        out_specs=[vm] * 4,
        scratch_shapes=[
            pltpu.VMEM((4 * TOK, MODEL), BF),
            pltpu.VMEM((4 * HEAD, MODEL), BF),
            pltpu.VMEM((4 * TOK, 4 * HEAD), F32),
            pltpu.SemaphoreType.DMA((MODEL // CHUNK, 5)),
            pltpu.SemaphoreType.DMA((MODEL // CHUNK, 5)),
        ],
        compiler_params=pltpu.CompilerParams(vmem_limit_bytes=40 * 1024 * 1024),
        cost_estimate=pl.CostEstimate(flops=1, bytes_accessed=1, transcendentals=0),
        name="head_blocks",
    )(at, *g, *w, o)


def term_kernel(at, *refs):
    g, (o, mine, *other, gs, acc, gsem) = refs[:5], refs[5:]
    y, core = at[1], at[2]
    g_pieces = grad_pieces(y, *g)
    copies = [chunk_copies(g_pieces, gs, gsem, c) for c in range(MODEL // CHUNK)]
    for group in copies:
        for copy in group:
            copy.start()
    outs = o[...].reshape(4 * TOK, 4 * HEAD)
    for c, group in enumerate(copies):
        for copy in group:
            copy.wait()
        acc[pl.ds(c * CHUNK, CHUNK), :] = tn(gs[:, pl.ds(c * CHUNK, CHUNK)], outs)
    for z in range(8):
        mine[z] = acc[pl.ds(pl.multiple_of(400 * z + 200 * core, 8), 200), :].astype(BF)
        other[z // 2][z % 2] = acc[pl.ds(pl.multiple_of(400 * z + 200 - 200 * core, 8), 200), :].astype(BF)


def weight_term(at, g, o):
    vm = pl.BlockSpec(memory_space=pltpu.VMEM)
    sm = pl.BlockSpec(memory_space=pltpu.SMEM)
    hbm = pl.BlockSpec(memory_space=pl.ANY)
    return pl.pallas_call(
        term_kernel,
        out_shape=[jax.ShapeDtypeStruct((n, 200, 4 * HEAD), BF) for n in (8, 2, 2, 2, 2)],
        in_specs=[sm] + [hbm] * 5 + [vm],
        out_specs=[vm] * 5,
        scratch_shapes=[
            pltpu.VMEM((4 * TOK, MODEL), BF),
            pltpu.VMEM((MODEL, 4 * HEAD), F32),
            pltpu.SemaphoreType.DMA((MODEL // CHUNK, 5)),
        ],
        compiler_params=pltpu.CompilerParams(vmem_limit_bytes=40 * 1024 * 1024),
        cost_estimate=pl.CostEstimate(flops=1, bytes_accessed=1, transcendentals=0),
        name="weight_term",
    )(at, *g, o)


def pair_kernel(at, mine, *refs):
    other, outs = refs[:4], refs[4:]
    for k in range(4):
        cols = pl.ds(pl.multiple_of(lax.rem(at[0] + k, 4) * HEAD, HEAD), HEAD)
        for z in range(8):
            outs[k][z] = (mine[z, :, cols].astype(F32) + other[z // 2][z % 2, :, cols].astype(F32)).astype(BF)


def pair_sum(at, mine, *other):
    vm = pl.BlockSpec(memory_space=pltpu.VMEM)
    sm = pl.BlockSpec(memory_space=pltpu.SMEM)
    return pl.pallas_call(
        pair_kernel,
        out_shape=[jax.ShapeDtypeStruct((8, 200, HEAD), BF)] * 4,
        in_specs=[sm] + [vm] * 5,
        out_specs=[vm] * 4,
        cost_estimate=pl.CostEstimate(flops=1, bytes_accessed=1, transcendentals=0),
        name="pair_sum",
    )(at, mine, *other)


def row_kernel(at, a, b, c, d, kept, sent):
    bit = lax.rem(at[3], 2)
    for i in range(4):
        own, away = 2 * i + bit, 2 * i + 1 - bit
        kept[i] = a[own].astype(F32) + b[own].astype(F32) + c[own].astype(F32) + d[own].astype(F32)
        sent[i] = (a[away].astype(F32) + b[away].astype(F32) + c[away].astype(F32) + d[away].astype(F32)).astype(BF)


def half_kernel(shift, at, held, got, kept, sent):
    bit = lax.rem(lax.div(at[3], shift), 2)
    for i in range(held.shape[0] // 2):
        own, away = 2 * i + bit, 2 * i + 1 - bit
        kept[i] = held[own] + got[own].astype(F32)
        sent[i] = (held[away] + got[away].astype(F32)).astype(BF)


def halved(at, parts, shift, count):
    vm = pl.BlockSpec(memory_space=pltpu.VMEM)
    sm = pl.BlockSpec(memory_space=pltpu.SMEM)
    body = row_kernel if shift == 1 else lambda *refs: half_kernel(shift, *refs)
    return pl.pallas_call(
        body,
        out_shape=[jax.ShapeDtypeStruct((count, 200, HEAD), F32), jax.ShapeDtypeStruct((count, 200, HEAD), BF)],
        in_specs=[sm] + [vm] * len(parts),
        out_specs=[vm] * 2,
        cost_estimate=pl.CostEstimate(flops=2300000000, bytes_accessed=7200000, transcendentals=0),
        name=f"halved_{shift}",
    )(at, *parts)


def last_kernel(held, got, out):
    out[...] = (held[0] + got[0].astype(F32)).T * (1.0 / math.sqrt(PACK * 16))


def last_sum(held, got):
    vm = pl.BlockSpec(memory_space=pltpu.VMEM)
    return pl.pallas_call(
        last_kernel,
        out_shape=jax.ShapeDtypeStruct((HEAD, 200), F32),
        in_specs=[vm] * 2,
        out_specs=vm,
        cost_estimate=pl.CostEstimate(flops=2300000000, bytes_accessed=7200000, transcendentals=0),
        name="last_sum",
    )(held, got)


def on_device(queries, keys_in, values_in, saved_out, out_grad, out_weight, image_units):
    seq = lax.axis_index("seq").astype(jnp.int32)
    dp = lax.axis_index("dp").astype(jnp.int32)
    core = lax.rem(dp, 2)
    at = jnp.stack([lax.div(seq, 4), lax.rem(seq, 4), core, lax.div(dp, 2)])
    after = lax.optimization_barrier
    move = lax.ppermute

    g = out_grad[0]
    back, ahead = move(g, "seq", YS[1]), move(g, "seq", YS[3])
    wa = move(out_weight, ("dp", "seq"), BOTH)
    wc = move(lax.dynamic_slice_in_dim(out_weight, 64 * core, 64, 0), "seq", XS[2])
    o_rows = lax.all_to_all(
        pack_out(saved_out[0]), "seq", split_axis=0, concat_axis=0, tiled=True, axis_index_groups=YGROUPS
    )
    back, ahead, wa, wc, o_rows = after((back, ahead, wa, wc, o_rows))
    fa, fb = move(back[:64], "seq", YS[1]), move(ahead[64:], "seq", YS[3])
    wb, wd = move(wa, "dp", CORES), move(wc, "dp", CORES)
    g_pieces = (g, back, ahead, fa, fb)
    heads = head_blocks(at, g_pieces, (out_weight, wa, wb, wc, wd), o_rows)
    local, o_later = after((heads[0], o_rows))
    heads = [local] + [move(heads[k], "seq", XS[4 - k]) for k in (1, 2, 3)]

    packed, _, _, _, _ = after((pack(queries[0], keys_in[0], values_in[0]), fa, fb, wb, wd))
    qkv = lax.all_to_all(packed, "seq", split_axis=0, concat_axis=0, tiled=True)
    mine, *other = weight_term(at, g_pieces, o_later)
    pairs = pair_sum(at, mine, *[move(part, "dp", CORES) for part in other])
    qkv, *pairs = after((qkv, *pairs))
    grads = attention(at, image_units[0], qkv, heads)
    sent = lax.all_to_all(grads, "seq", split_axis=0, concat_axis=0, tiled=True)
    query_grad, key_grad, value_grad = unpack(sent)

    parts = [pairs[0]] + [move(pairs[k], "seq", XS[k]) for k in (1, 2, 3)]
    held, away = halved(at, parts, 1, 4)
    held, away = halved(at, [held, move(away, "dp", ZS[0])], 2, 2)
    held, away = halved(at, [held, move(away, "dp", ZS[1])], 4, 1)
    weight_grad = last_sum(held, move(away, "dp", ZS[2]))
    return query_grad[None], key_grad[None], value_grad[None], weight_grad


def solution(mesh):
    rows = P("dp", "seq", None)
    return jax.shard_map(
        on_device,
        mesh=mesh,
        in_specs=(rows, rows, rows, rows, rows, P("seq", None), P("dp", None)),
        out_specs=(rows, rows, rows, P("seq", "dp")),
        check_vma=False,
    )
```

```python
import math

import jax
import jax.numpy as jnp
from jax import lax
from jax.experimental import pallas as pl
from jax.experimental.pallas import tpu as pltpu
from jax.sharding import PartitionSpec as P

HEAD = 128
PACK = 2048
TOK = 128
MODEL = 3200
IMG = 512
SEGS = 8
NEG = -1e30
BF = jnp.bfloat16
F32 = jnp.float32
XS = [[(4 * x + y, 4 * ((x + k) % 4) + y) for x in range(4) for y in range(4)] for k in range(4)]
YS = [[(4 * x + y, 4 * x + (y + k) % 4) for x in range(4) for y in range(4)] for k in range(4)]
YGROUPS = [[4 * x + y for y in range(4)] for x in range(4)]
CORES = [(i, i ^ 1) for i in range(16)]
ZNEAR = [(2 * z + c, 2 * (z ^ 1) + c) for z in range(8) for c in range(2)]
ZFAR = [[(2 * z + c, 2 * ((z + 2 * k) % 8) + c) for z in range(8) for c in range(2)] for k in range(4)]
BOTH = [
    (16 * d + 4 * x + y, 16 * d + 4 * ((x + (1, 3)[d % 2]) % 4) + y)
    for d in range(16)
    for x in range(4)
    for y in range(4)
]
CHUNK = 640


def nt(a, b):
    return lax.dot_general(a, b, (((1,), (1,)), ((), ())), preferred_element_type=F32)


def nn(a, b):
    return lax.dot_general(a, b, (((1,), (0,)), ((), ())), preferred_element_type=F32)


def tn(a, b):
    return lax.dot_general(a, b, (((0,), (0,)), ((), ())), preferred_element_type=F32)


def attention_kernel(xi, units, qkv, h0, h1, h2, h3, out, qs, ks, vs, hs, ds_, gq, gk, gv):
    for i in range(16):
        rows = pl.ds(i * TOK, TOK)
        qs[rows, :] = qkv[i, 0]
        ks[rows, :] = qkv[i, 1]
        vs[rows, :] = qkv[i, 2]
    tail = pl.ds(PACK, IMG)
    for ref in (qs, ks, vs, hs):
        ref[tail, :] = jnp.zeros((IMG, HEAD), BF)
    ds_[pl.ds(16, 8), :] = jnp.zeros((8, HEAD), F32)
    for k, h in enumerate((h0, h1, h2, h3)):
        block = lax.rem(xi[0] + k, 4)
        hs[pl.ds(pl.multiple_of(block * IMG, IMG), IMG), :] = h[pl.ds(0, IMG), :]
        parts = h[pl.ds(IMG, 16), :].astype(F32)
        ds_[pl.ds(block * 4, 4), :] = parts[0:4] + parts[4:8] + parts[8:12]
    scaling = 1.0 / math.sqrt(HEAD)
    to_two = scaling * math.log2(math.e)

    def image(start, size, width, step):
        kw = ks[pl.ds(start, width), :]
        vw = vs[pl.ds(start, width), :]
        row = lax.broadcasted_iota(jnp.int32, (width, 1), 0)
        bias = jnp.where(row < size, 0.0, NEG).astype(F32)
        first = lax.div(start, TOK)
        shift = start - first * TOK
        gk_sum = gv_sum = None
        for b in range(width // step):
            here = pl.ds(pl.multiple_of(start + b * step, 16), step)
            qb = qs[here, :]
            hb = hs[here, :]
            lane = lax.broadcasted_iota(jnp.int32, (1, step), 1) + b * step
            pieces = []
            for n in range(step // TOK):
                line = first + b * (step // TOK) + n
                two = jnp.concatenate([ds_[pl.ds(line, 1), :], ds_[pl.ds(line + 1, 1), :]], axis=1)
                pieces.append(pltpu.roll(two, 2 * TOK - shift, 1)[:, :TOK])
            delta = pieces[0] if len(pieces) == 1 else jnp.concatenate(pieces, axis=1)
            s = nt(kw, qb) * to_two + bias
            top = jnp.max(s, axis=0, keepdims=True)
            e = jnp.exp2(s - top)
            norm = jnp.where(lane < size, 1.0 / jnp.sum(e, axis=0, keepdims=True), 0.0)
            p = e * norm
            dp = nt(vw, hb)
            dsc = (p * (dp - delta)).astype(BF)
            pk = nn(dsc, qb)
            pv = nn(p.astype(BF), hb)
            gk_sum = pk if gk_sum is None else gk_sum + pk
            gv_sum = pv if gv_sum is None else gv_sum + pv
            gq[here, :] = (tn(dsc, kw) * scaling).astype(BF)
        gk[pl.ds(start, width), :] = (gk_sum * scaling).astype(BF)
        gv[pl.ds(start, width), :] = gv_sum.astype(BF)

    def one(j, start):
        size = units[j] * 16
        start = pl.multiple_of(start, 16)
        for width, step in ((128, 128), (256, 256), (384, 384), (512, 512)):
            pl.when((size > width - 128) & (size <= width))(lambda width=width, step=step: image(start, size, width, step))
        return start + size

    lax.fori_loop(0, SEGS, one, jnp.int32(0))
    for i in range(16):
        rows = pl.ds(i * TOK, TOK)
        out[i, 0] = gq[rows, :]
        out[i, 1] = gk[rows, :]
        out[i, 2] = gv[rows, :]


def attention(xi, units, qkv, hs):
    vm = pl.BlockSpec(memory_space=pltpu.VMEM)
    sm = pl.BlockSpec(memory_space=pltpu.SMEM)
    return pl.pallas_call(
        attention_kernel,
        out_shape=jax.ShapeDtypeStruct((16, 3, TOK, HEAD), BF),
        in_specs=[sm, sm] + [vm] * 5,
        out_specs=vm,
        scratch_shapes=[pltpu.VMEM((PACK + IMG, HEAD), BF)] * 4 + [pltpu.VMEM((24, HEAD), F32)] + [pltpu.VMEM((PACK + IMG, HEAD), BF)] * 3,
        compiler_params=pltpu.CompilerParams(vmem_limit_bytes=60 * 1024 * 1024),
        cost_estimate=pl.CostEstimate(flops=10350000000, bytes_accessed=32400000, transcendentals=0),
        name="attention",
    )(xi, units, qkv, *hs)


def pack_kernel(q, k, v, out):
    for i in range(16):
        cols = pl.ds(i * HEAD, HEAD)
        out[i, 0] = q[:, cols]
        out[i, 1] = k[:, cols]
        out[i, 2] = v[:, cols]


def pack(q, k, v):
    vm = pl.BlockSpec(memory_space=pltpu.VMEM)
    return pl.pallas_call(
        pack_kernel,
        out_shape=jax.ShapeDtypeStruct((16, 3, TOK, HEAD), BF),
        in_specs=[vm] * 3,
        out_specs=vm,
        cost_estimate=pl.CostEstimate(flops=1150000, bytes_accessed=3600, transcendentals=0),
        name="pack",
    )(q, k, v)


def unpack_kernel(grads, q, k, v):
    for i in range(16):
        cols = pl.ds(i * HEAD, HEAD)
        q[:, cols] = grads[i, 0]
        k[:, cols] = grads[i, 1]
        v[:, cols] = grads[i, 2]


def unpack(grads):
    rows = TOK // 2
    return pl.pallas_call(
        unpack_kernel,
        grid=(2,),
        out_shape=[jax.ShapeDtypeStruct((TOK, 16 * HEAD), BF)] * 3,
        in_specs=[pl.BlockSpec((16, 3, rows, HEAD), lambda i: (0, 0, i, 0))],
        out_specs=[pl.BlockSpec((rows, 16 * HEAD), lambda i: (i, 0))] * 3,
        compiler_params=pltpu.CompilerParams(vmem_limit_bytes=60 * 1024 * 1024),
        cost_estimate=pl.CostEstimate(flops=1, bytes_accessed=1, transcendentals=0),
        name="unpack",
    )(grads)


def three_terms(value):
    high = value.astype(BF)
    rest = value - high.astype(F32)
    middle = rest.astype(BF)
    return jnp.concatenate([high, middle, (rest - middle.astype(F32)).astype(BF), jnp.zeros_like(high)], axis=0)


def pack_out_kernel(o, out):
    for y in range(4):
        for x in range(4):
            out[y, :, pl.ds(x * HEAD, HEAD)] = o[:, pl.ds((4 * x + y) * HEAD, HEAD)]


def pack_out(o):
    vm = pl.BlockSpec(memory_space=pltpu.VMEM)
    return pl.pallas_call(
        pack_out_kernel,
        out_shape=jax.ShapeDtypeStruct((4, TOK, 4 * HEAD), BF),
        in_specs=[vm],
        out_specs=vm,
        cost_estimate=pl.CostEstimate(flops=1, bytes_accessed=1, transcendentals=0),
        name="pack_out",
    )(o)


def chunk_copies(pieces, whole, sems, c):
    cols = pl.ds(c * CHUNK, CHUNK)
    copies = []
    for n, (ref, row) in enumerate(pieces):
        rows = ref.shape[0]
        copies.append(
            pltpu.make_async_copy(
                ref.at[:, cols], whole.at[pl.ds(pl.multiple_of(row, 64), rows), cols], sems.at[c, n]
            )
        )
    return copies


def grad_pieces(y, g, back, ahead, fa, fb):
    far = lax.rem(y + 2, 4) * TOK
    return [(g, y * TOK), (back, lax.rem(y + 3, 4) * TOK), (ahead, lax.rem(y + 1, 4) * TOK), (fa, far), (fb, far + 64)]


def head_kernel(at, *refs):
    g, (w, wa, wb, wc, wd, o), hs, (gs, ws, acc, gsem, wsem) = refs[:5], refs[5:11], refs[11:15], refs[15:]
    x, y, core = at[0], at[1], at[2]
    g_pieces = grad_pieces(y, *g)
    near = lax.select(core == 0, 1, 3)
    w_pieces = [
        (w, 0),
        (wa, near * TOK),
        (wb, (4 - near) * TOK),
        (wc, 2 * TOK + 64 * core),
        (wd, 2 * TOK + 64 * (1 - core)),
    ]
    copies = [chunk_copies(w_pieces, ws, wsem, c) + chunk_copies(g_pieces, gs, gsem, c) for c in range(MODEL // CHUNK)]
    for group in copies:
        for copy in group:
            copy.start()
    for c, group in enumerate(copies):
        for copy in group:
            copy.wait()
        cols = pl.ds(c * CHUNK, CHUNK)
        part = nt(gs[:, cols], ws[:, cols])
        if c == 0:
            acc[...] = part
        else:
            acc[...] += part
    for k in range(4):
        own = pl.ds(pl.multiple_of(lax.rem(x + 4 - k, 4) * HEAD, HEAD), HEAD)
        lines = []
        for j in range(4):
            rows = pl.ds(j * TOK, TOK)
            h = acc[rows, pl.ds(k * HEAD, HEAD)].astype(BF)
            hs[k][rows, :] = h
            product = h.astype(F32) * o[j, :, own].astype(F32)
            lines.append(jnp.sum(product.T, axis=0, keepdims=True))
        hs[k][pl.ds(4 * TOK, 16), :] = three_terms(jnp.concatenate(lines, axis=0))


def head_blocks(at, g, w, o):
    vm = pl.BlockSpec(memory_space=pltpu.VMEM)
    sm = pl.BlockSpec(memory_space=pltpu.SMEM)
    hbm = pl.BlockSpec(memory_space=pl.ANY)
    return pl.pallas_call(
        head_kernel,
        out_shape=[jax.ShapeDtypeStruct((4 * TOK + 16, HEAD), BF)] * 4,
        in_specs=[sm] + [hbm] * 10 + [vm],
        out_specs=[vm] * 4,
        scratch_shapes=[
            pltpu.VMEM((4 * TOK, MODEL), BF),
            pltpu.VMEM((4 * HEAD, MODEL), BF),
            pltpu.VMEM((4 * TOK, 4 * HEAD), F32),
            pltpu.SemaphoreType.DMA((MODEL // CHUNK, 5)),
            pltpu.SemaphoreType.DMA((MODEL // CHUNK, 5)),
        ],
        compiler_params=pltpu.CompilerParams(vmem_limit_bytes=60 * 1024 * 1024),
        cost_estimate=pl.CostEstimate(flops=3450000000, bytes_accessed=10800000, transcendentals=0),
        name="head_blocks",
    )(at, *g, *w, o)


def term_kernel(at, *refs):
    g, (o, mine, *other, gs, acc, gsem) = refs[:5], refs[5:]
    y, core = at[1], at[2]
    g_pieces = grad_pieces(y, *g)
    copies = [chunk_copies(g_pieces, gs, gsem, c) for c in range(MODEL // CHUNK)]
    for group in copies:
        for copy in group:
            copy.start()
    outs = o[...].reshape(4 * TOK, 4 * HEAD)
    for c, group in enumerate(copies):
        for copy in group:
            copy.wait()
        acc[pl.ds(c * CHUNK, CHUNK), :] = tn(gs[:, pl.ds(c * CHUNK, CHUNK)], outs)
    for z in range(8):
        mine[z] = acc[pl.ds(pl.multiple_of(400 * z + 200 * core, 8), 200), :].astype(BF)
        other[z // 2][z % 2] = acc[pl.ds(pl.multiple_of(400 * z + 200 - 200 * core, 8), 200), :].astype(BF)


def weight_term(at, g, o):
    vm = pl.BlockSpec(memory_space=pltpu.VMEM)
    sm = pl.BlockSpec(memory_space=pltpu.SMEM)
    hbm = pl.BlockSpec(memory_space=pl.ANY)
    return pl.pallas_call(
        term_kernel,
        out_shape=[jax.ShapeDtypeStruct((n, 200, 4 * HEAD), BF) for n in (8, 2, 2, 2, 2)],
        in_specs=[sm] + [hbm] * 5 + [vm],
        out_specs=[vm] * 5,
        scratch_shapes=[
            pltpu.VMEM((4 * TOK, MODEL), BF),
            pltpu.VMEM((MODEL, 4 * HEAD), F32),
            pltpu.SemaphoreType.DMA((MODEL // CHUNK, 5)),
        ],
        compiler_params=pltpu.CompilerParams(vmem_limit_bytes=60 * 1024 * 1024),
        cost_estimate=pl.CostEstimate(flops=6900000000, bytes_accessed=21600000, transcendentals=0),
        name="weight_term",
    )(at, *g, o)


def pair_kernel(at, mine, *refs):
    other, outs = refs[:4], refs[4:]
    for k in range(4):
        cols = pl.ds(pl.multiple_of(lax.rem(at[0] + k, 4) * HEAD, HEAD), HEAD)
        for z in range(8):
            outs[k][z] = (mine[z, :, cols].astype(F32) + other[z // 2][z % 2, :, cols].astype(F32)).astype(BF)


def pair_sum(at, mine, *other):
    vm = pl.BlockSpec(memory_space=pltpu.VMEM)
    sm = pl.BlockSpec(memory_space=pltpu.SMEM)
    return pl.pallas_call(
        pair_kernel,
        out_shape=[jax.ShapeDtypeStruct((8, 200, HEAD), BF)] * 4,
        in_specs=[sm] + [vm] * 5,
        out_specs=[vm] * 4,
        cost_estimate=pl.CostEstimate(flops=1, bytes_accessed=1, transcendentals=0),
        name="pair_sum",
    )(at, mine, *other)


def on_device(queries, keys_in, values_in, saved_out, out_grad, out_weight, image_units):
    seq = lax.axis_index("seq").astype(jnp.int32)
    dp = lax.axis_index("dp").astype(jnp.int32)
    core, z = lax.rem(dp, 2), lax.div(dp, 2)
    at = jnp.stack([lax.div(seq, 4), lax.rem(seq, 4), core, z])
    after = lax.optimization_barrier
    move = lax.ppermute

    g = out_grad[0]
    back, ahead = move(g, "seq", YS[1]), move(g, "seq", YS[3])
    wa = move(out_weight, ("dp", "seq"), BOTH)
    wc = move(lax.dynamic_slice_in_dim(out_weight, 64 * core, 64, 0), "seq", XS[2])
    o_rows = lax.all_to_all(
        pack_out(saved_out[0]), "seq", split_axis=0, concat_axis=0, tiled=True, axis_index_groups=YGROUPS
    )
    back, ahead, wa, wc, o_rows = after((back, ahead, wa, wc, o_rows))
    q, fa, fb = after((queries[0], back[:64], ahead[64:]))
    fa, fb = move(fa, "seq", YS[1]), move(fb, "seq", YS[3])
    wb, wd = move(wa, "dp", CORES), move(wc, "dp", CORES)
    qkv = lax.all_to_all(pack(q, keys_in[0], values_in[0]), "seq", split_axis=0, concat_axis=0, tiled=True)
    g_pieces = (g, back, ahead, fa, fb)

    mine, *other = weight_term(at, g_pieces, o_rows)
    mine, at_later = after((mine, at))
    heads = head_blocks(at_later, g_pieces, (out_weight, wa, wb, wc, wd), o_rows)
    heads = [heads[0]] + [move(heads[k], "seq", XS[4 - k]) for k in (1, 2, 3)]

    pairs = pair_sum(at, mine, *[move(part, "dp", CORES) for part in other])
    qkv, *pairs = after((qkv, *pairs))
    grads = attention(at, image_units[0], qkv, heads)
    sent = lax.all_to_all(grads, "seq", split_axis=0, concat_axis=0, tiled=True)
    query_grad, key_grad, value_grad = unpack(sent)

    total = pairs[0].astype(F32)
    for k in (1, 2, 3):
        total = total + move(pairs[k], "seq", XS[k]).astype(F32)
    total = total.reshape(4, 2, 200, HEAD)
    bit, quarter = lax.rem(z, 2), lax.div(z, 2)
    away = lax.dynamic_index_in_dim(total, 1 - bit, 1, keepdims=False).astype(BF)
    total = lax.dynamic_index_in_dim(total, bit, 1, keepdims=False) + move(away, "dp", ZNEAR).astype(F32)
    last = lax.dynamic_index_in_dim(total, quarter, 0, keepdims=False)
    for k in (1, 2, 3):
        part = lax.dynamic_index_in_dim(total, lax.rem(quarter + k, 4), 0, keepdims=False).astype(BF)
        last = last + move(part, "dp", ZFAR[k]).astype(F32)
    weight_grad = last.T * (1.0 / math.sqrt(PACK * 16))
    return query_grad[None], key_grad[None], value_grad[None], weight_grad


def solution(mesh):
    rows = P("dp", "seq", None)
    return jax.shard_map(
        on_device,
        mesh=mesh,
        in_specs=(rows, rows, rows, rows, rows, P("seq", None), P("dp", None)),
        out_specs=(rows, rows, rows, P("seq", "dp")),
        check_vma=False,
    )
```

```python
import math

import jax
import jax.numpy as jnp
from jax import lax
from jax.experimental import pallas as pl
from jax.experimental.pallas import tpu as pltpu
from jax.sharding import PartitionSpec as P

HEAD = 128
PACK = 2048
TOK = 128
MODEL = 3200
IMG = 512
SEGS = 8
NEG = -1e30
BF = jnp.bfloat16
F32 = jnp.float32
XS = [[(4 * x + y, 4 * ((x + k) % 4) + y) for x in range(4) for y in range(4)] for k in range(4)]
YS = [[(4 * x + y, 4 * x + (y + k) % 4) for x in range(4) for y in range(4)] for k in range(4)]
YGROUPS = [[4 * x + y for y in range(4)] for x in range(4)]
CORES = [(i, i ^ 1) for i in range(16)]
ZNEAR = [(2 * z + c, 2 * (z ^ 1) + c) for z in range(8) for c in range(2)]
ZFAR = [[(2 * z + c, 2 * ((z + 2 * k) % 8) + c) for z in range(8) for c in range(2)] for k in range(4)]
BOTH = [
    (16 * d + 4 * x + y, 16 * d + 4 * ((x + (1, 3)[d % 2]) % 4) + y)
    for d in range(16)
    for x in range(4)
    for y in range(4)
]
CHUNK = 640


def nt(a, b):
    return lax.dot_general(a, b, (((1,), (1,)), ((), ())), preferred_element_type=F32)


def nn(a, b):
    return lax.dot_general(a, b, (((1,), (0,)), ((), ())), preferred_element_type=F32)


def tn(a, b):
    return lax.dot_general(a, b, (((0,), (0,)), ((), ())), preferred_element_type=F32)


def attention_kernel(xi, units, qkv, h0, h1, h2, h3, out, qs, ks, vs, hs, ds_, gq, gk, gv):
    for i in range(16):
        rows = pl.ds(i * TOK, TOK)
        qs[rows, :] = qkv[i, 0]
        ks[rows, :] = qkv[i, 1]
        vs[rows, :] = qkv[i, 2]
    tail = pl.ds(PACK, IMG)
    for ref in (qs, ks, vs, hs):
        ref[tail, :] = jnp.zeros((IMG, HEAD), BF)
    ds_[pl.ds(16, 8), :] = jnp.zeros((8, HEAD), F32)
    for k, h in enumerate((h0, h1, h2, h3)):
        block = lax.rem(xi[0] + k, 4)
        hs[pl.ds(pl.multiple_of(block * IMG, IMG), IMG), :] = h[pl.ds(0, IMG), :]
        parts = h[pl.ds(IMG, 16), :].astype(F32)
        ds_[pl.ds(block * 4, 4), :] = parts[0:4] + parts[4:8] + parts[8:12]
    scaling = 1.0 / math.sqrt(HEAD)
    to_two = scaling * math.log2(math.e)

    def image(start, size, width, step):
        kw = ks[pl.ds(start, width), :]
        vw = vs[pl.ds(start, width), :]
        row = lax.broadcasted_iota(jnp.int32, (width, 1), 0)
        bias = jnp.where(row < size, 0.0, NEG).astype(F32)
        first = lax.div(start, TOK)
        shift = start - first * TOK
        gk_sum = gv_sum = None
        for b in range(width // step):
            here = pl.ds(pl.multiple_of(start + b * step, 16), step)
            qb = qs[here, :]
            hb = hs[here, :]
            lane = lax.broadcasted_iota(jnp.int32, (1, step), 1) + b * step
            pieces = []
            for n in range(step // TOK):
                line = first + b * (step // TOK) + n
                two = jnp.concatenate([ds_[pl.ds(line, 1), :], ds_[pl.ds(line + 1, 1), :]], axis=1)
                pieces.append(pltpu.roll(two, 2 * TOK - shift, 1)[:, :TOK])
            delta = pieces[0] if len(pieces) == 1 else jnp.concatenate(pieces, axis=1)
            s = nt(kw, qb) * to_two + bias
            top = jnp.max(s, axis=0, keepdims=True)
            e = jnp.exp2(s - top)
            norm = jnp.where(lane < size, 1.0 / jnp.sum(e, axis=0, keepdims=True), 0.0)
            p = e * norm
            dp = nt(vw, hb)
            dsc = (p * (dp - delta)).astype(BF)
            pk = nn(dsc, qb)
            pv = nn(p.astype(BF), hb)
            gk_sum = pk if gk_sum is None else gk_sum + pk
            gv_sum = pv if gv_sum is None else gv_sum + pv
            gq[here, :] = (tn(dsc, kw) * scaling).astype(BF)
        gk[pl.ds(start, width), :] = (gk_sum * scaling).astype(BF)
        gv[pl.ds(start, width), :] = gv_sum.astype(BF)

    def one(j, start):
        size = units[j] * 16
        start = pl.multiple_of(start, 16)
        for width, step in ((128, 128), (256, 256), (384, 384), (512, 512)):
            pl.when((size > width - 128) & (size <= width))(lambda width=width, step=step: image(start, size, width, step))
        return start + size

    lax.fori_loop(0, SEGS, one, jnp.int32(0))
    for i in range(16):
        rows = pl.ds(i * TOK, TOK)
        out[i, 0] = gq[rows, :]
        out[i, 1] = gk[rows, :]
        out[i, 2] = gv[rows, :]


def attention(xi, units, qkv, hs):
    vm = pl.BlockSpec(memory_space=pltpu.VMEM)
    sm = pl.BlockSpec(memory_space=pltpu.SMEM)
    return pl.pallas_call(
        attention_kernel,
        out_shape=jax.ShapeDtypeStruct((16, 3, TOK, HEAD), BF),
        in_specs=[sm, sm] + [vm] * 5,
        out_specs=vm,
        scratch_shapes=[pltpu.VMEM((PACK + IMG, HEAD), BF)] * 4 + [pltpu.VMEM((24, HEAD), F32)] + [pltpu.VMEM((PACK + IMG, HEAD), BF)] * 3,
        compiler_params=pltpu.CompilerParams(vmem_limit_bytes=60 * 1024 * 1024),
        cost_estimate=pl.CostEstimate(flops=10350000000, bytes_accessed=32400000, transcendentals=0),
        name="attention",
    )(xi, units, qkv, *hs)


def pack_kernel(q, k, v, out):
    for i in range(16):
        cols = pl.ds(i * HEAD, HEAD)
        out[i, 0] = q[:, cols]
        out[i, 1] = k[:, cols]
        out[i, 2] = v[:, cols]


def pack(q, k, v):
    vm = pl.BlockSpec(memory_space=pltpu.VMEM)
    return pl.pallas_call(
        pack_kernel,
        out_shape=jax.ShapeDtypeStruct((16, 3, TOK, HEAD), BF),
        in_specs=[vm] * 3,
        out_specs=vm,
        cost_estimate=pl.CostEstimate(flops=1150000, bytes_accessed=3600, transcendentals=0),
        name="pack",
    )(q, k, v)


def unpack_kernel(grads, q, k, v):
    for i in range(16):
        cols = pl.ds(i * HEAD, HEAD)
        q[:, cols] = grads[i, 0]
        k[:, cols] = grads[i, 1]
        v[:, cols] = grads[i, 2]


def unpack(grads):
    rows = TOK // 2
    return pl.pallas_call(
        unpack_kernel,
        grid=(2,),
        out_shape=[jax.ShapeDtypeStruct((TOK, 16 * HEAD), BF)] * 3,
        in_specs=[pl.BlockSpec((16, 3, rows, HEAD), lambda i: (0, 0, i, 0))],
        out_specs=[pl.BlockSpec((rows, 16 * HEAD), lambda i: (i, 0))] * 3,
        compiler_params=pltpu.CompilerParams(vmem_limit_bytes=63 * 1024 * 1024),
        cost_estimate=pl.CostEstimate(flops=1, bytes_accessed=1, transcendentals=0),
        name="unpack",
    )(grads)


def three_terms(value):
    high = value.astype(BF)
    rest = value - high.astype(F32)
    middle = rest.astype(BF)
    return jnp.concatenate([high, middle, (rest - middle.astype(F32)).astype(BF), jnp.zeros_like(high)], axis=0)


def pack_out_kernel(o, out):
    for y in range(4):
        for x in range(4):
            out[y, :, pl.ds(x * HEAD, HEAD)] = o[:, pl.ds((4 * x + y) * HEAD, HEAD)]


def pack_out(o):
    vm = pl.BlockSpec(memory_space=pltpu.VMEM)
    return pl.pallas_call(
        pack_out_kernel,
        out_shape=jax.ShapeDtypeStruct((4, TOK, 4 * HEAD), BF),
        in_specs=[vm],
        out_specs=vm,
        cost_estimate=pl.CostEstimate(flops=1, bytes_accessed=1, transcendentals=0),
        name="pack_out",
    )(o)


def chunk_copies(pieces, whole, sems, c):
    cols = pl.ds(c * CHUNK, CHUNK)
    copies = []
    for n, (ref, row) in enumerate(pieces):
        rows = ref.shape[0]
        copies.append(
            pltpu.make_async_copy(
                ref.at[:, cols], whole.at[pl.ds(pl.multiple_of(row, 64), rows), cols], sems.at[c, n]
            )
        )
    return copies


def grad_pieces(y, g, back, ahead, fa, fb):
    far = lax.rem(y + 2, 4) * TOK
    return [(g, y * TOK), (back, lax.rem(y + 3, 4) * TOK), (ahead, lax.rem(y + 1, 4) * TOK), (fa, far), (fb, far + 64)]


def block_kernel(at, *refs):
    g, (w, wa, wb, wc, wd, o), (mine, *other), hs = refs[:5], refs[5:11], refs[11:16], refs[16:20]
    gs, ws, term, acc, gsem, wsem = refs[20:]
    x, y, core = at[0], at[1], at[2]
    g_pieces = grad_pieces(y, *g)
    near = lax.select(core == 0, 1, 3)
    w_pieces = [
        (w, 0),
        (wa, near * TOK),
        (wb, (4 - near) * TOK),
        (wc, 2 * TOK + 64 * core),
        (wd, 2 * TOK + 64 * (1 - core)),
    ]
    g_copies = [chunk_copies(g_pieces, gs, gsem, c) for c in range(MODEL // CHUNK)]
    w_copies = [chunk_copies(w_pieces, ws, wsem, c) for c in range(MODEL // CHUNK)]
    for pair in zip(g_copies, w_copies):
        for copy in pair[0] + pair[1]:
            copy.start()
    outs = o[...].reshape(4 * TOK, 4 * HEAD)
    for c in range(MODEL // CHUNK):
        cols = pl.ds(c * CHUNK, CHUNK)
        for copy in g_copies[c]:
            copy.wait()
        term[cols, :] = tn(gs[:, cols], outs)
        for copy in w_copies[c]:
            copy.wait()
        part = nt(gs[:, cols], ws[:, cols])
        if c == 0:
            acc[...] = part
        else:
            acc[...] += part
    for k in range(4):
        own = pl.ds(pl.multiple_of(lax.rem(x + 4 - k, 4) * HEAD, HEAD), HEAD)
        lines = []
        for j in range(4):
            rows = pl.ds(j * TOK, TOK)
            h = acc[rows, pl.ds(k * HEAD, HEAD)].astype(BF)
            hs[k][rows, :] = h
            product = h.astype(F32) * o[j, :, own].astype(F32)
            lines.append(jnp.sum(product.T, axis=0, keepdims=True))
        hs[k][pl.ds(4 * TOK, 16), :] = three_terms(jnp.concatenate(lines, axis=0))
    for z in range(8):
        mine[z] = term[pl.ds(pl.multiple_of(400 * z + 200 * core, 8), 200), :].astype(BF)
        other[z // 2][z % 2] = term[pl.ds(pl.multiple_of(400 * z + 200 - 200 * core, 8), 200), :].astype(BF)


def blocks(at, g, w, o):
    vm = pl.BlockSpec(memory_space=pltpu.VMEM)
    sm = pl.BlockSpec(memory_space=pltpu.SMEM)
    hbm = pl.BlockSpec(memory_space=pl.ANY)
    sizes = [(n, 200, 4 * HEAD) for n in (8, 2, 2, 2, 2)] + [(4 * TOK + 16, HEAD)] * 4
    return pl.pallas_call(
        block_kernel,
        out_shape=[jax.ShapeDtypeStruct(size, BF) for size in sizes],
        in_specs=[sm] + [hbm] * 10 + [vm],
        out_specs=[vm] * 9,
        scratch_shapes=[
            pltpu.VMEM((4 * TOK, MODEL), BF),
            pltpu.VMEM((4 * HEAD, MODEL), BF),
            pltpu.VMEM((MODEL, 4 * HEAD), F32),
            pltpu.VMEM((4 * TOK, 4 * HEAD), F32),
            pltpu.SemaphoreType.DMA((MODEL // CHUNK, 5)),
            pltpu.SemaphoreType.DMA((MODEL // CHUNK, 5)),
        ],
        compiler_params=pltpu.CompilerParams(vmem_limit_bytes=60 * 1024 * 1024),
        cost_estimate=pl.CostEstimate(flops=10350000000, bytes_accessed=32400000, transcendentals=0),
        name="blocks",
    )(at, *g, *w, o)


def pair_kernel(at, mine, *refs):
    other, outs = refs[:4], refs[4:]
    for k in range(4):
        cols = pl.ds(pl.multiple_of(lax.rem(at[0] + k, 4) * HEAD, HEAD), HEAD)
        for z in range(8):
            outs[k][z] = (mine[z, :, cols].astype(F32) + other[z // 2][z % 2, :, cols].astype(F32)).astype(BF)


def pair_sum(at, mine, *other):
    vm = pl.BlockSpec(memory_space=pltpu.VMEM)
    sm = pl.BlockSpec(memory_space=pltpu.SMEM)
    return pl.pallas_call(
        pair_kernel,
        out_shape=[jax.ShapeDtypeStruct((8, 200, HEAD), BF)] * 4,
        in_specs=[sm] + [vm] * 5,
        out_specs=[vm] * 4,
        cost_estimate=pl.CostEstimate(flops=1, bytes_accessed=1, transcendentals=0),
        name="pair_sum",
    )(at, mine, *other)


def on_device(queries, keys_in, values_in, saved_out, out_grad, out_weight, image_units):
    seq = lax.axis_index("seq").astype(jnp.int32)
    dp = lax.axis_index("dp").astype(jnp.int32)
    core, z = lax.rem(dp, 2), lax.div(dp, 2)
    at = jnp.stack([lax.div(seq, 4), lax.rem(seq, 4), core, z])
    after = lax.optimization_barrier
    move = lax.ppermute

    g = out_grad[0]
    back, ahead = move(g, "seq", YS[1]), move(g, "seq", YS[3])
    wa = move(out_weight, ("dp", "seq"), BOTH)
    wc = move(lax.dynamic_slice_in_dim(out_weight, 64 * core, 64, 0), "seq", XS[2])
    o_rows = lax.all_to_all(
        pack_out(saved_out[0]), "seq", split_axis=0, concat_axis=0, tiled=True, axis_index_groups=YGROUPS
    )
    back, ahead, wa, wc, o_rows = after((back, ahead, wa, wc, o_rows))
    q, fa, fb = after((queries[0], back[:64], ahead[64:]))
    fa, fb = move(fa, "seq", YS[1]), move(fb, "seq", YS[3])
    wb, wd = move(wa, "dp", CORES), move(wc, "dp", CORES)
    qkv = lax.all_to_all(pack(q, keys_in[0], values_in[0]), "seq", split_axis=0, concat_axis=0, tiled=True)
    g_pieces = (g, back, ahead, fa, fb)

    mine, *other, h0, h1, h2, h3 = blocks(at, g_pieces, (out_weight, wa, wb, wc, wd), o_rows)
    heads = [h0] + [move(h, "seq", XS[4 - k]) for k, h in ((1, h1), (2, h2), (3, h3))]

    pairs = pair_sum(at, mine, *[move(part, "dp", CORES) for part in other])
    qkv, *pairs = after((qkv, *pairs))
    grads = attention(at, image_units[0], qkv, heads)
    sent = lax.all_to_all(grads, "seq", split_axis=0, concat_axis=0, tiled=True)
    query_grad, key_grad, value_grad = unpack(sent)

    total = pairs[0].astype(F32)
    for k in (1, 2, 3):
        total = total + move(pairs[k], "seq", XS[k]).astype(F32)
    total = total.reshape(4, 2, 200, HEAD)
    bit, quarter = lax.rem(z, 2), lax.div(z, 2)
    away = lax.dynamic_index_in_dim(total, 1 - bit, 1, keepdims=False).astype(BF)
    total = lax.dynamic_index_in_dim(total, bit, 1, keepdims=False) + move(away, "dp", ZNEAR).astype(F32)
    last = lax.dynamic_index_in_dim(total, quarter, 0, keepdims=False)
    for k in (1, 2, 3):
        part = lax.dynamic_index_in_dim(total, lax.rem(quarter + k, 4), 0, keepdims=False).astype(BF)
        last = last + move(part, "dp", ZFAR[k]).astype(F32)
    weight_grad = last.T * (1.0 / math.sqrt(PACK * 16))
    return query_grad[None], key_grad[None], value_grad[None], weight_grad


def solution(mesh):
    rows = P("dp", "seq", None)
    return jax.shard_map(
        on_device,
        mesh=mesh,
        in_specs=(rows, rows, rows, rows, rows, P("seq", None), P("dp", None)),
        out_specs=(rows, rows, rows, P("seq", "dp")),
        check_vma=False,
    )
```

```python
import math

import jax
import jax.numpy as jnp
from jax import lax
from jax.experimental import pallas as pl
from jax.experimental.pallas import tpu as pltpu
from jax.sharding import PartitionSpec as P

HEAD = 128
PACK = 2048
TOK = 128
MODEL = 3200
IMG = 512
SEGS = 8
NEG = -1e30
BF = jnp.bfloat16
F32 = jnp.float32
XS = [[(4 * x + y, 4 * ((x + k) % 4) + y) for x in range(4) for y in range(4)] for k in range(4)]
YS = [[(4 * x + y, 4 * x + (y + k) % 4) for x in range(4) for y in range(4)] for k in range(4)]
YGROUPS = [[4 * x + y for y in range(4)] for x in range(4)]
CORES = [(i, i ^ 1) for i in range(16)]
ZNEAR = [(2 * z + c, 2 * (z ^ 1) + c) for z in range(8) for c in range(2)]
ZFAR = [[(2 * z + c, 2 * ((z + 2 * k) % 8) + c) for z in range(8) for c in range(2)] for k in range(4)]
BOTH = [
    (16 * d + 4 * x + y, 16 * d + 4 * ((x + (1, 3)[d % 2]) % 4) + y)
    for d in range(16)
    for x in range(4)
    for y in range(4)
]
CHUNK = 640


def nt(a, b):
    return lax.dot_general(a, b, (((1,), (1,)), ((), ())), preferred_element_type=F32)


def nn(a, b):
    return lax.dot_general(a, b, (((1,), (0,)), ((), ())), preferred_element_type=F32)


def tn(a, b):
    return lax.dot_general(a, b, (((0,), (0,)), ((), ())), preferred_element_type=F32)


def attention_kernel(xi, units, qkv, h0, h1, h2, h3, out, qs, ks, vs, hs, ds_, gq, gk, gv):
    for i in range(16):
        rows = pl.ds(i * TOK, TOK)
        qs[rows, :] = qkv[i, 0]
        ks[rows, :] = qkv[i, 1]
        vs[rows, :] = qkv[i, 2]
    tail = pl.ds(PACK, IMG)
    for ref in (qs, ks, vs, hs):
        ref[tail, :] = jnp.zeros((IMG, HEAD), BF)
    ds_[pl.ds(16, 8), :] = jnp.zeros((8, HEAD), F32)
    for k, h in enumerate((h0, h1, h2, h3)):
        block = lax.rem(xi[0] + k, 4)
        hs[pl.ds(pl.multiple_of(block * IMG, IMG), IMG), :] = h[pl.ds(0, IMG), :]
        parts = h[pl.ds(IMG, 16), :].astype(F32)
        ds_[pl.ds(block * 4, 4), :] = parts[0:4] + parts[4:8] + parts[8:12]
    scaling = 1.0 / math.sqrt(HEAD)
    to_two = scaling * math.log2(math.e)

    def image(start, size, width, step):
        kw = ks[pl.ds(start, width), :]
        vw = vs[pl.ds(start, width), :]
        row = lax.broadcasted_iota(jnp.int32, (width, 1), 0)
        bias = jnp.where(row < size, 0.0, NEG).astype(F32)
        first = lax.div(start, TOK)
        shift = start - first * TOK
        gk_sum = gv_sum = None
        for b in range(width // step):
            here = pl.ds(pl.multiple_of(start + b * step, 16), step)
            qb = qs[here, :]
            hb = hs[here, :]
            lane = lax.broadcasted_iota(jnp.int32, (1, step), 1) + b * step
            pieces = []
            for n in range(step // TOK):
                line = first + b * (step // TOK) + n
                two = jnp.concatenate([ds_[pl.ds(line, 1), :], ds_[pl.ds(line + 1, 1), :]], axis=1)
                pieces.append(pltpu.roll(two, 2 * TOK - shift, 1)[:, :TOK])
            delta = pieces[0] if len(pieces) == 1 else jnp.concatenate(pieces, axis=1)
            s = nt(kw, qb) * to_two + bias
            top = jnp.max(s, axis=0, keepdims=True)
            e = jnp.exp2(s - top)
            norm = jnp.where(lane < size, 1.0 / jnp.sum(e, axis=0, keepdims=True), 0.0)
            p = e * norm
            dp = nt(vw, hb)
            dsc = (p * (dp - delta)).astype(BF)
            pk = nn(dsc, qb)
            pv = nn(p.astype(BF), hb)
            gk_sum = pk if gk_sum is None else gk_sum + pk
            gv_sum = pv if gv_sum is None else gv_sum + pv
            gq[here, :] = (tn(dsc, kw) * scaling).astype(BF)
        gk[pl.ds(start, width), :] = (gk_sum * scaling).astype(BF)
        gv[pl.ds(start, width), :] = gv_sum.astype(BF)

    def one(j, start):
        size = units[j] * 16
        start = pl.multiple_of(start, 16)
        for width, step in ((128, 128), (256, 256), (384, 384), (512, 512)):
            pl.when((size > width - 128) & (size <= width))(lambda width=width, step=step: image(start, size, width, step))
        return start + size

    lax.fori_loop(0, SEGS, one, jnp.int32(0))
    for i in range(16):
        rows = pl.ds(i * TOK, TOK)
        out[i, 0] = gq[rows, :]
        out[i, 1] = gk[rows, :]
        out[i, 2] = gv[rows, :]


def attention(xi, units, qkv, hs):
    vm = pl.BlockSpec(memory_space=pltpu.VMEM)
    sm = pl.BlockSpec(memory_space=pltpu.SMEM)
    return pl.pallas_call(
        attention_kernel,
        out_shape=jax.ShapeDtypeStruct((16, 3, TOK, HEAD), BF),
        in_specs=[sm, sm] + [vm] * 5,
        out_specs=vm,
        scratch_shapes=[pltpu.VMEM((PACK + IMG, HEAD), BF)] * 4 + [pltpu.VMEM((24, HEAD), F32)] + [pltpu.VMEM((PACK + IMG, HEAD), BF)] * 3,
        compiler_params=pltpu.CompilerParams(vmem_limit_bytes=32 * 1024 * 1024),
        cost_estimate=pl.CostEstimate(flops=10350000000, bytes_accessed=32400000, transcendentals=0),
        name="attention",
    )(xi, units, qkv, *hs)


def pack_kernel(q, k, v, out):
    for i in range(16):
        cols = pl.ds(i * HEAD, HEAD)
        out[i, 0] = q[:, cols]
        out[i, 1] = k[:, cols]
        out[i, 2] = v[:, cols]


def pack(q, k, v):
    vm = pl.BlockSpec(memory_space=pltpu.VMEM)
    return pl.pallas_call(
        pack_kernel,
        out_shape=jax.ShapeDtypeStruct((16, 3, TOK, HEAD), BF),
        in_specs=[vm] * 3,
        out_specs=vm,
        cost_estimate=pl.CostEstimate(flops=1150000, bytes_accessed=3600, transcendentals=0),
        name="pack",
    )(q, k, v)


def unpack_kernel(grads, q, k, v):
    for i in range(16):
        cols = pl.ds(i * HEAD, HEAD)
        q[:, cols] = grads[i, 0]
        k[:, cols] = grads[i, 1]
        v[:, cols] = grads[i, 2]


def unpack(grads):
    rows = TOK // 2
    return pl.pallas_call(
        unpack_kernel,
        grid=(2,),
        out_shape=[jax.ShapeDtypeStruct((TOK, 16 * HEAD), BF)] * 3,
        in_specs=[pl.BlockSpec((16, 3, rows, HEAD), lambda i: (0, 0, i, 0))],
        out_specs=[pl.BlockSpec((rows, 16 * HEAD), lambda i: (i, 0))] * 3,
        compiler_params=pltpu.CompilerParams(vmem_limit_bytes=63 * 1024 * 1024),
        cost_estimate=pl.CostEstimate(flops=1, bytes_accessed=1, transcendentals=0),
        name="unpack",
    )(grads)


def three_terms(value):
    high = value.astype(BF)
    rest = value - high.astype(F32)
    middle = rest.astype(BF)
    return jnp.concatenate([high, middle, (rest - middle.astype(F32)).astype(BF), jnp.zeros_like(high)], axis=0)


def pack_out_kernel(o, out):
    for y in range(4):
        for x in range(4):
            out[y, :, pl.ds(x * HEAD, HEAD)] = o[:, pl.ds((4 * x + y) * HEAD, HEAD)]


def pack_out(o):
    vm = pl.BlockSpec(memory_space=pltpu.VMEM)
    return pl.pallas_call(
        pack_out_kernel,
        out_shape=jax.ShapeDtypeStruct((4, TOK, 4 * HEAD), BF),
        in_specs=[vm],
        out_specs=vm,
        cost_estimate=pl.CostEstimate(flops=1, bytes_accessed=1, transcendentals=0),
        name="pack_out",
    )(o)


def chunk_copies(pieces, whole, sems, c):
    cols = pl.ds(c * CHUNK, CHUNK)
    copies = []
    for n, (ref, row) in enumerate(pieces):
        rows = ref.shape[0]
        copies.append(
            pltpu.make_async_copy(
                ref.at[:, cols], whole.at[pl.ds(pl.multiple_of(row, 64), rows), cols], sems.at[c, n]
            )
        )
    return copies


def grad_pieces(y, g, back, ahead, fa, fb):
    far = lax.rem(y + 2, 4) * TOK
    return [(g, y * TOK), (back, lax.rem(y + 3, 4) * TOK), (ahead, lax.rem(y + 1, 4) * TOK), (fa, far), (fb, far + 64)]


def block_kernel(at, *refs):
    g, (w, wa, wb, wc, wd, o), (mine, *other), hs = refs[:5], refs[5:11], refs[11:16], refs[16:20]
    gs, ws, term, staged, acc, gsem, wsem, osem = refs[20:]
    x, y, core = at[0], at[1], at[2]
    g_pieces = grad_pieces(y, *g)
    near = lax.select(core == 0, 1, 3)
    w_pieces = [
        (w, 0),
        (wa, near * TOK),
        (wb, (4 - near) * TOK),
        (wc, 2 * TOK + 64 * core),
        (wd, 2 * TOK + 64 * (1 - core)),
    ]
    g_copies = [chunk_copies(g_pieces, gs, gsem, c) for c in range(MODEL // CHUNK)]
    w_copies = [chunk_copies(w_pieces, ws, wsem, c) for c in range(MODEL // CHUNK)]
    for pair in zip(g_copies, w_copies):
        for copy in pair[0] + pair[1]:
            copy.start()
    outs = o[...].reshape(4 * TOK, 4 * HEAD)
    for c in range(MODEL // CHUNK):
        cols = pl.ds(c * CHUNK, CHUNK)
        for copy in g_copies[c]:
            copy.wait()
        term[cols, :] = tn(gs[:, cols], outs)
        for m in range(CHUNK * c // 200, CHUNK * (c + 1) // 200):
            staged[m] = term[pl.ds(200 * m, 200), :].astype(BF)
            z = m // 2
            inside = staged.at[m], mine.at[z], osem.at[m]
            outside = staged.at[m], other[z // 2].at[z % 2], osem.at[m]
            pl.when(core == m % 2)(lambda refs=inside: pltpu.make_async_copy(*refs).start())
            pl.when(core != m % 2)(lambda refs=outside: pltpu.make_async_copy(*refs).start())
        for copy in w_copies[c]:
            copy.wait()
        part = nt(gs[:, cols], ws[:, cols])
        if c == 0:
            acc[...] = part
        else:
            acc[...] += part
    for k in range(4):
        own = pl.ds(pl.multiple_of(lax.rem(x + 4 - k, 4) * HEAD, HEAD), HEAD)
        lines = []
        for j in range(4):
            rows = pl.ds(j * TOK, TOK)
            h = acc[rows, pl.ds(k * HEAD, HEAD)].astype(BF)
            hs[k][rows, :] = h
            product = h.astype(F32) * o[j, :, own].astype(F32)
            lines.append(jnp.sum(product.T, axis=0, keepdims=True))
        hs[k][pl.ds(4 * TOK, 16), :] = three_terms(jnp.concatenate(lines, axis=0))
    for m in range(16):
        pltpu.make_async_copy(staged.at[m], mine.at[m // 2], osem.at[m]).wait()


def blocks(at, g, w, o):
    vm = pl.BlockSpec(memory_space=pltpu.VMEM)
    sm = pl.BlockSpec(memory_space=pltpu.SMEM)
    hbm = pl.BlockSpec(memory_space=pl.ANY)
    sizes = [(n, 200, 4 * HEAD) for n in (8, 2, 2, 2, 2)] + [(4 * TOK + 16, HEAD)] * 4
    return pl.pallas_call(
        block_kernel,
        out_shape=[jax.ShapeDtypeStruct(size, BF) for size in sizes],
        in_specs=[sm] + [hbm] * 10 + [vm],
        out_specs=[hbm] * 5 + [vm] * 4,
        scratch_shapes=[
            pltpu.VMEM((4 * TOK, MODEL), BF),
            pltpu.VMEM((4 * HEAD, MODEL), BF),
            pltpu.VMEM((MODEL, 4 * HEAD), F32),
            pltpu.VMEM((16, 200, 4 * HEAD), BF),
            pltpu.VMEM((4 * TOK, 4 * HEAD), F32),
            pltpu.SemaphoreType.DMA((MODEL // CHUNK, 5)),
            pltpu.SemaphoreType.DMA((MODEL // CHUNK, 5)),
            pltpu.SemaphoreType.DMA((16,)),
        ],
        compiler_params=pltpu.CompilerParams(vmem_limit_bytes=60 * 1024 * 1024),
        cost_estimate=pl.CostEstimate(flops=10350000000, bytes_accessed=32400000, transcendentals=0),
        name="blocks",
    )(at, *g, *w, o)


def pair_kernel(at, mine, *refs):
    other, outs = refs[:4], refs[4:]
    for k in range(4):
        cols = pl.ds(pl.multiple_of(lax.rem(at[0] + k, 4) * HEAD, HEAD), HEAD)
        for z in range(8):
            outs[k][z] = (mine[z, :, cols].astype(F32) + other[z // 2][z % 2, :, cols].astype(F32)).astype(BF)


def pair_sum(at, mine, *other):
    vm = pl.BlockSpec(memory_space=pltpu.VMEM)
    sm = pl.BlockSpec(memory_space=pltpu.SMEM)
    return pl.pallas_call(
        pair_kernel,
        out_shape=[jax.ShapeDtypeStruct((8, 200, HEAD), BF)] * 4,
        in_specs=[sm] + [vm] * 5,
        out_specs=[vm] * 4,
        cost_estimate=pl.CostEstimate(flops=1, bytes_accessed=1, transcendentals=0),
        name="pair_sum",
    )(at, mine, *other)


def on_device(queries, keys_in, values_in, saved_out, out_grad, out_weight, image_units):
    seq = lax.axis_index("seq").astype(jnp.int32)
    dp = lax.axis_index("dp").astype(jnp.int32)
    core, z = lax.rem(dp, 2), lax.div(dp, 2)
    at = jnp.stack([lax.div(seq, 4), lax.rem(seq, 4), core, z])
    after = lax.optimization_barrier
    move = lax.ppermute

    g = out_grad[0]
    back, ahead = move(g, "seq", YS[1]), move(g, "seq", YS[3])
    wa = move(out_weight, ("dp", "seq"), BOTH)
    wc = move(lax.dynamic_slice_in_dim(out_weight, 64 * core, 64, 0), "seq", XS[2])
    o_rows = lax.all_to_all(
        pack_out(saved_out[0]), "seq", split_axis=0, concat_axis=0, tiled=True, axis_index_groups=YGROUPS
    )
    back, ahead, wa, wc, o_rows = after((back, ahead, wa, wc, o_rows))
    q, fa, fb = after((queries[0], back[:64], ahead[64:]))
    fa, fb = move(fa, "seq", YS[1]), move(fb, "seq", YS[3])
    wb, wd = move(wa, "dp", CORES), move(wc, "dp", CORES)
    qkv = lax.all_to_all(pack(q, keys_in[0], values_in[0]), "seq", split_axis=0, concat_axis=0, tiled=True)
    g_pieces = (g, back, ahead, fa, fb)

    mine, *other, h0, h1, h2, h3 = blocks(at, g_pieces, (out_weight, wa, wb, wc, wd), o_rows)
    heads = [h0] + [move(h, "seq", XS[4 - k]) for k, h in ((1, h1), (2, h2), (3, h3))]

    pairs = pair_sum(at, mine, *[move(part, "dp", CORES) for part in other])
    qkv, *_ = after((qkv, *pairs))
    grads = attention(at, image_units[0], qkv, heads)
    sent = lax.all_to_all(grads, "seq", split_axis=0, concat_axis=0, tiled=True)
    query_grad, key_grad, value_grad = unpack(sent)

    total = pairs[0].astype(F32)
    for k in (1, 2, 3):
        total = total + move(pairs[k], "seq", XS[k]).astype(F32)
    total = total.reshape(4, 2, 200, HEAD)
    bit, quarter = lax.rem(z, 2), lax.div(z, 2)
    away = lax.dynamic_index_in_dim(total, 1 - bit, 1, keepdims=False).astype(BF)
    total = lax.dynamic_index_in_dim(total, bit, 1, keepdims=False) + move(away, "dp", ZNEAR).astype(F32)
    parts = [lax.dynamic_index_in_dim(total, quarter, 0, keepdims=False)]
    for k in (1, 2, 3):
        part = lax.dynamic_index_in_dim(total, lax.rem(quarter + k, 4), 0, keepdims=False).astype(BF)
        parts.append(move(part, "dp", ZFAR[k]))
    *parts, query_grad, key_grad, value_grad = after((*parts, query_grad, key_grad, value_grad))
    last = sum([part.astype(F32) for part in parts[1:]], parts[0])
    weight_grad = last.T * (1.0 / math.sqrt(PACK * 16))
    return query_grad[None], key_grad[None], value_grad[None], weight_grad


def solution(mesh):
    rows = P("dp", "seq", None)
    return jax.shard_map(
        on_device,
        mesh=mesh,
        in_specs=(rows, rows, rows, rows, rows, P("seq", None), P("dp", None)),
        out_specs=(rows, rows, rows, P("seq", "dp")),
        check_vma=False,
    )
```

```python
import math

import jax
import jax.numpy as jnp
from jax import lax
from jax.experimental import pallas as pl
from jax.experimental.pallas import tpu as pltpu
from jax.sharding import PartitionSpec as P

HEAD = 128
PACK = 2048
TOK = 128
MODEL = 3200
IMG = 512
SEGS = 8
NEG = -1e30
BF = jnp.bfloat16
F32 = jnp.float32
XS = [[(4 * x + y, 4 * ((x + k) % 4) + y) for x in range(4) for y in range(4)] for k in range(4)]
YS = [[(4 * x + y, 4 * x + (y + k) % 4) for x in range(4) for y in range(4)] for k in range(4)]
YGROUPS = [[4 * x + y for y in range(4)] for x in range(4)]
CORES = [(i, i ^ 1) for i in range(16)]
ZNEAR = [(2 * z + c, 2 * (z ^ 1) + c) for z in range(8) for c in range(2)]
ZFAR = [[(2 * z + c, 2 * ((z + 2 * k) % 8) + c) for z in range(8) for c in range(2)] for k in range(4)]
BOTH = [
    (16 * d + 4 * x + y, 16 * d + 4 * ((x + (1, 3)[d % 2]) % 4) + y)
    for d in range(16)
    for x in range(4)
    for y in range(4)
]
CHUNK = 640


def nt(a, b):
    return lax.dot_general(a, b, (((1,), (1,)), ((), ())), preferred_element_type=F32)


def nn(a, b):
    return lax.dot_general(a, b, (((1,), (0,)), ((), ())), preferred_element_type=F32)


def tn(a, b):
    return lax.dot_general(a, b, (((0,), (0,)), ((), ())), preferred_element_type=F32)


def attention_kernel(xi, units, qkv, h0, h1, h2, h3, out, qs, ks, vs, hs, ds_, gq, gk, gv):
    for i in range(16):
        rows = pl.ds(i * TOK, TOK)
        qs[rows, :] = qkv[i, 0]
        ks[rows, :] = qkv[i, 1]
        vs[rows, :] = qkv[i, 2]
    tail = pl.ds(PACK, IMG)
    for ref in (qs, ks, vs, hs):
        ref[tail, :] = jnp.zeros((IMG, HEAD), BF)
    ds_[pl.ds(16, 8), :] = jnp.zeros((8, HEAD), F32)
    for k, h in enumerate((h0, h1, h2, h3)):
        block = lax.rem(xi[0] + k, 4)
        hs[pl.ds(pl.multiple_of(block * IMG, IMG), IMG), :] = h[pl.ds(0, IMG), :]
        parts = h[pl.ds(IMG, 16), :].astype(F32)
        ds_[pl.ds(block * 4, 4), :] = parts[0:4] + parts[4:8] + parts[8:12]
    scaling = 1.0 / math.sqrt(HEAD)
    to_two = scaling * math.log2(math.e)

    def image(start, size, width, step):
        kw = ks[pl.ds(start, width), :]
        vw = vs[pl.ds(start, width), :]
        row = lax.broadcasted_iota(jnp.int32, (width, 1), 0)
        bias = jnp.where(row < size, 0.0, NEG).astype(F32)
        first = lax.div(start, TOK)
        shift = start - first * TOK
        gk_sum = gv_sum = None
        for b in range(width // step):
            here = pl.ds(pl.multiple_of(start + b * step, 16), step)
            qb = qs[here, :]
            hb = hs[here, :]
            lane = lax.broadcasted_iota(jnp.int32, (1, step), 1) + b * step
            pieces = []
            for n in range(step // TOK):
                line = first + b * (step // TOK) + n
                two = jnp.concatenate([ds_[pl.ds(line, 1), :], ds_[pl.ds(line + 1, 1), :]], axis=1)
                pieces.append(pltpu.roll(two, 2 * TOK - shift, 1)[:, :TOK])
            delta = pieces[0] if len(pieces) == 1 else jnp.concatenate(pieces, axis=1)
            s = nt(kw, qb) * to_two + bias
            top = jnp.max(s, axis=0, keepdims=True)
            e = jnp.exp2(s - top)
            norm = jnp.where(lane < size, 1.0 / jnp.sum(e, axis=0, keepdims=True), 0.0)
            p = e * norm
            dp = nt(vw, hb)
            dsc = (p * (dp - delta)).astype(BF)
            pk = nn(dsc, qb)
            pv = nn(p.astype(BF), hb)
            gk_sum = pk if gk_sum is None else gk_sum + pk
            gv_sum = pv if gv_sum is None else gv_sum + pv
            gq[here, :] = (tn(dsc, kw) * scaling).astype(BF)
        gk[pl.ds(start, width), :] = (gk_sum * scaling).astype(BF)
        gv[pl.ds(start, width), :] = gv_sum.astype(BF)

    def one(j, start):
        size = units[j] * 16
        start = pl.multiple_of(start, 16)
        for width, step in ((128, 128), (256, 256), (384, 384), (512, 512)):
            pl.when((size > width - 128) & (size <= width))(lambda width=width, step=step: image(start, size, width, step))
        return start + size

    lax.fori_loop(0, SEGS, one, jnp.int32(0))
    for i in range(16):
        rows = pl.ds(i * TOK, TOK)
        out[i, 0] = gq[rows, :]
        out[i, 1] = gk[rows, :]
        out[i, 2] = gv[rows, :]


def attention(xi, units, qkv, hs):
    vm = pl.BlockSpec(memory_space=pltpu.VMEM)
    sm = pl.BlockSpec(memory_space=pltpu.SMEM)
    return pl.pallas_call(
        attention_kernel,
        out_shape=jax.ShapeDtypeStruct((16, 3, TOK, HEAD), BF),
        in_specs=[sm, sm] + [vm] * 5,
        out_specs=vm,
        scratch_shapes=[pltpu.VMEM((PACK + IMG, HEAD), BF)] * 4 + [pltpu.VMEM((24, HEAD), F32)] + [pltpu.VMEM((PACK + IMG, HEAD), BF)] * 3,
        compiler_params=pltpu.CompilerParams(vmem_limit_bytes=24 * 1024 * 1024),
        cost_estimate=pl.CostEstimate(flops=10350000000, bytes_accessed=32400000, transcendentals=0),
        name="attention",
    )(xi, units, qkv, *hs)


def pack_kernel(q, k, v, out):
    for i in range(16):
        cols = pl.ds(i * HEAD, HEAD)
        out[i, 0] = q[:, cols]
        out[i, 1] = k[:, cols]
        out[i, 2] = v[:, cols]


def pack(q, k, v):
    vm = pl.BlockSpec(memory_space=pltpu.VMEM)
    return pl.pallas_call(
        pack_kernel,
        out_shape=jax.ShapeDtypeStruct((16, 3, TOK, HEAD), BF),
        in_specs=[vm] * 3,
        out_specs=vm,
        cost_estimate=pl.CostEstimate(flops=1150000, bytes_accessed=3600, transcendentals=0),
        name="pack",
    )(q, k, v)


def unpack_kernel(grads, q, k, v):
    for i in range(16):
        cols = pl.ds(i * HEAD, HEAD)
        q[:, cols] = grads[i, 0]
        k[:, cols] = grads[i, 1]
        v[:, cols] = grads[i, 2]


def unpack(grads):
    rows = TOK // 2
    return pl.pallas_call(
        unpack_kernel,
        grid=(2,),
        out_shape=[jax.ShapeDtypeStruct((TOK, 16 * HEAD), BF)] * 3,
        in_specs=[pl.BlockSpec((16, 3, rows, HEAD), lambda i: (0, 0, i, 0))],
        out_specs=[pl.BlockSpec((rows, 16 * HEAD), lambda i: (i, 0))] * 3,
        compiler_params=pltpu.CompilerParams(vmem_limit_bytes=63 * 1024 * 1024),
        cost_estimate=pl.CostEstimate(flops=1, bytes_accessed=1, transcendentals=0),
        name="unpack",
    )(grads)


def three_terms(value):
    high = value.astype(BF)
    rest = value - high.astype(F32)
    middle = rest.astype(BF)
    return jnp.concatenate([high, middle, (rest - middle.astype(F32)).astype(BF), jnp.zeros_like(high)], axis=0)


def pack_out_kernel(o, out):
    for y in range(4):
        for x in range(4):
            out[y, :, pl.ds(x * HEAD, HEAD)] = o[:, pl.ds((4 * x + y) * HEAD, HEAD)]


def pack_out(o):
    vm = pl.BlockSpec(memory_space=pltpu.VMEM)
    return pl.pallas_call(
        pack_out_kernel,
        out_shape=jax.ShapeDtypeStruct((4, TOK, 4 * HEAD), BF),
        in_specs=[vm],
        out_specs=vm,
        cost_estimate=pl.CostEstimate(flops=1, bytes_accessed=1, transcendentals=0),
        name="pack_out",
    )(o)


def chunk_copies(pieces, whole, sems, c):
    cols = pl.ds(c * CHUNK, CHUNK)
    copies = []
    for n, (ref, row) in enumerate(pieces):
        rows = ref.shape[0]
        copies.append(
            pltpu.make_async_copy(
                ref.at[:, cols], whole.at[pl.ds(pl.multiple_of(row, 64), rows), cols], sems.at[c, n]
            )
        )
    return copies


def grad_pieces(y, g, back, ahead, fa, fb):
    far = lax.rem(y + 2, 4) * TOK
    return [(g, y * TOK), (back, lax.rem(y + 3, 4) * TOK), (ahead, lax.rem(y + 1, 4) * TOK), (fa, far), (fb, far + 64)]


def block_kernel(at, *refs):
    g, (w, wa, wb, wc, wd, o), (mine, *other), hs = refs[:5], refs[5:11], refs[11:14], refs[14:18]
    gs, ws, term, staged, acc, gsem, wsem, osem = refs[18:]
    x, y, core = at[0], at[1], at[2]
    g_pieces = grad_pieces(y, *g)
    near = lax.select(core == 0, 1, 3)
    w_pieces = [
        (w, 0),
        (wa, near * TOK),
        (wb, (4 - near) * TOK),
        (wc, 2 * TOK + 64 * core),
        (wd, 2 * TOK + 64 * (1 - core)),
    ]
    g_copies = [chunk_copies(g_pieces, gs, gsem, c) for c in range(MODEL // CHUNK)]
    w_copies = [chunk_copies(w_pieces, ws, wsem, c) for c in range(MODEL // CHUNK)]
    for pair in zip(g_copies, w_copies):
        for copy in pair[0] + pair[1]:
            copy.start()
    outs = o[...].reshape(4 * TOK, 4 * HEAD)
    for c in range(MODEL // CHUNK):
        cols = pl.ds(c * CHUNK, CHUNK)
        for copy in g_copies[c]:
            copy.wait()
        term[cols, :] = tn(gs[:, cols], outs)
        for m in range(CHUNK * c // 200, CHUNK * (c + 1) // 200):
            staged[m] = term[pl.ds(200 * m, 200), :].astype(BF)
            z = m // 2
            inside = staged.at[m], mine.at[z], osem.at[m]
            outside = staged.at[m], other[z // 4].at[z % 4], osem.at[m]
            pl.when(core == m % 2)(lambda refs=inside: pltpu.make_async_copy(*refs).start())
            pl.when(core != m % 2)(lambda refs=outside: pltpu.make_async_copy(*refs).start())
        for copy in w_copies[c]:
            copy.wait()
        part = nt(gs[:, cols], ws[:, cols])
        if c == 0:
            acc[...] = part
        else:
            acc[...] += part
    for k in range(4):
        own = pl.ds(pl.multiple_of(lax.rem(x + 4 - k, 4) * HEAD, HEAD), HEAD)
        lines = []
        for j in range(4):
            rows = pl.ds(j * TOK, TOK)
            h = acc[rows, pl.ds(k * HEAD, HEAD)].astype(BF)
            hs[k][rows, :] = h
            product = h.astype(F32) * o[j, :, own].astype(F32)
            lines.append(jnp.sum(product.T, axis=0, keepdims=True))
        hs[k][pl.ds(4 * TOK, 16), :] = three_terms(jnp.concatenate(lines, axis=0))
    for m in range(16):
        pltpu.make_async_copy(staged.at[m], mine.at[m // 2], osem.at[m]).wait()


def blocks(at, g, w, o):
    vm = pl.BlockSpec(memory_space=pltpu.VMEM)
    sm = pl.BlockSpec(memory_space=pltpu.SMEM)
    hbm = pl.BlockSpec(memory_space=pl.ANY)
    sizes = [(n, 200, 4 * HEAD) for n in (8, 4, 4)] + [(4 * TOK + 16, HEAD)] * 4
    return pl.pallas_call(
        block_kernel,
        out_shape=[jax.ShapeDtypeStruct(size, BF) for size in sizes],
        in_specs=[sm] + [hbm] * 10 + [vm],
        out_specs=[hbm] * 3 + [vm] * 4,
        scratch_shapes=[
            pltpu.VMEM((4 * TOK, MODEL), BF),
            pltpu.VMEM((4 * HEAD, MODEL), BF),
            pltpu.VMEM((MODEL, 4 * HEAD), F32),
            pltpu.VMEM((16, 200, 4 * HEAD), BF),
            pltpu.VMEM((4 * TOK, 4 * HEAD), F32),
            pltpu.SemaphoreType.DMA((MODEL // CHUNK, 5)),
            pltpu.SemaphoreType.DMA((MODEL // CHUNK, 5)),
            pltpu.SemaphoreType.DMA((16,)),
        ],
        compiler_params=pltpu.CompilerParams(vmem_limit_bytes=60 * 1024 * 1024),
        cost_estimate=pl.CostEstimate(flops=10350000000, bytes_accessed=32400000, transcendentals=0),
        name="blocks",
    )(at, *g, *w, o)


def pair_kernel(at, mine, *refs):
    other, outs = refs[:2], refs[2:]
    for k in range(4):
        cols = pl.ds(pl.multiple_of(lax.rem(at[0] + k, 4) * HEAD, HEAD), HEAD)
        for z in range(8):
            outs[k][z] = (mine[z, :, cols].astype(F32) + other[z // 4][z % 4, :, cols].astype(F32)).astype(BF)


def pair_sum(at, mine, *other):
    vm = pl.BlockSpec(memory_space=pltpu.VMEM)
    sm = pl.BlockSpec(memory_space=pltpu.SMEM)
    return pl.pallas_call(
        pair_kernel,
        out_shape=[jax.ShapeDtypeStruct((8, 200, HEAD), BF)] * 4,
        in_specs=[sm] + [vm] * 3,
        out_specs=[vm] * 4,
        cost_estimate=pl.CostEstimate(flops=1, bytes_accessed=1, transcendentals=0),
        name="pair_sum",
    )(at, mine, *other)


def on_device(queries, keys_in, values_in, saved_out, out_grad, out_weight, image_units):
    seq = lax.axis_index("seq").astype(jnp.int32)
    dp = lax.axis_index("dp").astype(jnp.int32)
    core, z = lax.rem(dp, 2), lax.div(dp, 2)
    at = jnp.stack([lax.div(seq, 4), lax.rem(seq, 4), core, z])
    after = lax.optimization_barrier
    move = lax.ppermute

    g = out_grad[0]
    back, ahead = move(g, "seq", YS[1]), move(g, "seq", YS[3])
    wa = move(out_weight, ("dp", "seq"), BOTH)
    wc = move(lax.dynamic_slice_in_dim(out_weight, 64 * core, 64, 0), "seq", XS[2])
    o_rows = lax.all_to_all(
        pack_out(saved_out[0]), "seq", split_axis=0, concat_axis=0, tiled=True, axis_index_groups=YGROUPS
    )
    back, ahead, wa, wc, o_rows, at = after((back, ahead, wa, wc, o_rows, at))
    q, fa, fb = after((queries[0], back[:64], ahead[64:]))
    fa, fb = move(fa, "seq", YS[1]), move(fb, "seq", YS[3])
    wb, wd = move(wa, "dp", CORES), move(wc, "dp", CORES)
    qkv = lax.all_to_all(pack(q, keys_in[0], values_in[0]), "seq", split_axis=0, concat_axis=0, tiled=True)
    g_pieces = (g, back, ahead, fa, fb)

    mine, *other, h0, h1, h2, h3 = blocks(at, g_pieces, (out_weight, wa, wb, wc, wd), o_rows)
    heads = [h0] + [move(h, "seq", XS[4 - k]) for k, h in ((1, h1), (2, h2), (3, h3))]

    pairs = pair_sum(at, mine, *[move(part, "dp", CORES) for part in other])
    qkv, *_ = after((qkv, *pairs))
    grads = attention(at, image_units[0], qkv, heads)
    sent = lax.all_to_all(grads, "seq", split_axis=0, concat_axis=0, tiled=True)
    query_grad, key_grad, value_grad = unpack(sent)

    total = pairs[0].astype(F32)
    for k in (1, 2, 3):
        total = total + move(pairs[k], "seq", XS[k]).astype(F32)
    total = total.reshape(4, 2, 200, HEAD)
    bit, quarter = lax.rem(z, 2), lax.div(z, 2)
    away = lax.dynamic_index_in_dim(total, 1 - bit, 1, keepdims=False).astype(BF)
    total = lax.dynamic_index_in_dim(total, bit, 1, keepdims=False) + move(away, "dp", ZNEAR).astype(F32)
    parts = [lax.dynamic_index_in_dim(total, quarter, 0, keepdims=False)]
    for k in (1, 2, 3):
        part = lax.dynamic_index_in_dim(total, lax.rem(quarter + k, 4), 0, keepdims=False).astype(BF)
        parts.append(move(part, "dp", ZFAR[k]))
    *parts, query_grad, key_grad, value_grad = after((*parts, query_grad, key_grad, value_grad))
    last = sum([part.astype(F32) for part in parts[1:]], parts[0])
    weight_grad = last.T * (1.0 / math.sqrt(PACK * 16))
    return query_grad[None], key_grad[None], value_grad[None], weight_grad


def solution(mesh):
    rows = P("dp", "seq", None)
    return jax.shard_map(
        on_device,
        mesh=mesh,
        in_specs=(rows, rows, rows, rows, rows, P("seq", None), P("dp", None)),
        out_specs=(rows, rows, rows, P("seq", "dp")),
        check_vma=False,
    )
```

```python
import math

import jax
import jax.numpy as jnp
from jax import lax
from jax.experimental import pallas as pl
from jax.experimental.pallas import tpu as pltpu
from jax.sharding import PartitionSpec as P

HEAD = 128
PACK = 2048
TOK = 128
MODEL = 3200
IMG = 512
SEGS = 8
NEG = -1e30
BF = jnp.bfloat16
F32 = jnp.float32
XS = [[(4 * x + y, 4 * ((x + k) % 4) + y) for x in range(4) for y in range(4)] for k in range(4)]
YS = [[(4 * x + y, 4 * x + (y + k) % 4) for x in range(4) for y in range(4)] for k in range(4)]
YGROUPS = [[4 * x + y for y in range(4)] for x in range(4)]
CORES = [(i, i ^ 1) for i in range(16)]
ZNEAR = [(2 * z + c, 2 * (z ^ 1) + c) for z in range(8) for c in range(2)]
ZFAR = [[(2 * z + c, 2 * ((z + 2 * k) % 8) + c) for z in range(8) for c in range(2)] for k in range(4)]
BOTH = [
    (16 * d + 4 * x + y, 16 * d + 4 * ((x + (1, 3)[d % 2]) % 4) + y)
    for d in range(16)
    for x in range(4)
    for y in range(4)
]
CHUNK = 640


def nt(a, b):
    return lax.dot_general(a, b, (((1,), (1,)), ((), ())), preferred_element_type=F32)


def nn(a, b):
    return lax.dot_general(a, b, (((1,), (0,)), ((), ())), preferred_element_type=F32)


def tn(a, b):
    return lax.dot_general(a, b, (((0,), (0,)), ((), ())), preferred_element_type=F32)


def attention_kernel(xi, units, qkv, h0, h1, h2, h3, out, qs, ks, vs, hs, ds_, gq, gk, gv):
    for i in range(16):
        rows = pl.ds(i * TOK, TOK)
        qs[rows, :] = qkv[i, 0]
        ks[rows, :] = qkv[i, 1]
        vs[rows, :] = qkv[i, 2]
    tail = pl.ds(PACK, IMG)
    for ref in (qs, ks, vs, hs):
        ref[tail, :] = jnp.zeros((IMG, HEAD), BF)
    ds_[pl.ds(16, 8), :] = jnp.zeros((8, HEAD), F32)
    for k, h in enumerate((h0, h1, h2, h3)):
        block = lax.rem(xi[0] + k, 4)
        hs[pl.ds(pl.multiple_of(block * IMG, IMG), IMG), :] = h[pl.ds(0, IMG), :]
        parts = h[pl.ds(IMG, 16), :].astype(F32)
        ds_[pl.ds(block * 4, 4), :] = parts[0:4] + parts[4:8] + parts[8:12]
    scaling = 1.0 / math.sqrt(HEAD)
    to_two = scaling * math.log2(math.e)

    def image(start, size, width, step):
        kw = ks[pl.ds(start, width), :]
        vw = vs[pl.ds(start, width), :]
        row = lax.broadcasted_iota(jnp.int32, (width, 1), 0)
        bias = jnp.where(row < size, 0.0, NEG).astype(F32)
        first = lax.div(start, TOK)
        shift = start - first * TOK
        gk_sum = gv_sum = None
        for b in range(width // step):
            here = pl.ds(pl.multiple_of(start + b * step, 16), step)
            qb = qs[here, :]
            hb = hs[here, :]
            lane = lax.broadcasted_iota(jnp.int32, (1, step), 1) + b * step
            pieces = []
            for n in range(step // TOK):
                line = first + b * (step // TOK) + n
                two = jnp.concatenate([ds_[pl.ds(line, 1), :], ds_[pl.ds(line + 1, 1), :]], axis=1)
                pieces.append(pltpu.roll(two, 2 * TOK - shift, 1)[:, :TOK])
            delta = pieces[0] if len(pieces) == 1 else jnp.concatenate(pieces, axis=1)
            s = nt(kw, qb) * to_two + bias
            top = jnp.max(s, axis=0, keepdims=True)
            e = jnp.exp2(s - top)
            norm = jnp.where(lane < size, 1.0 / jnp.sum(e, axis=0, keepdims=True), 0.0)
            p = e * norm
            dp = nt(vw, hb)
            dsc = (p * (dp - delta)).astype(BF)
            pk = nn(dsc, qb)
            pv = nn(p.astype(BF), hb)
            gk_sum = pk if gk_sum is None else gk_sum + pk
            gv_sum = pv if gv_sum is None else gv_sum + pv
            gq[here, :] = (tn(dsc, kw) * scaling).astype(BF)
        gk[pl.ds(start, width), :] = (gk_sum * scaling).astype(BF)
        gv[pl.ds(start, width), :] = gv_sum.astype(BF)

    def one(j, start):
        size = units[j] * 16
        start = pl.multiple_of(start, 16)
        for width, step in ((128, 128), (256, 256), (384, 384), (512, 512)):
            pl.when((size > width - 128) & (size <= width))(lambda width=width, step=step: image(start, size, width, step))
        return start + size

    lax.fori_loop(0, SEGS, one, jnp.int32(0))
    for i in range(16):
        rows = pl.ds(i * TOK, TOK)
        out[i, 0] = gq[rows, :]
        out[i, 1] = gk[rows, :]
        out[i, 2] = gv[rows, :]


def attention(xi, units, qkv, hs):
    vm = pl.BlockSpec(memory_space=pltpu.VMEM)
    sm = pl.BlockSpec(memory_space=pltpu.SMEM)
    return pl.pallas_call(
        attention_kernel,
        out_shape=jax.ShapeDtypeStruct((16, 3, TOK, HEAD), BF),
        in_specs=[sm, sm] + [vm] * 5,
        out_specs=vm,
        scratch_shapes=[pltpu.VMEM((PACK + IMG, HEAD), BF)] * 4 + [pltpu.VMEM((24, HEAD), F32)] + [pltpu.VMEM((PACK + IMG, HEAD), BF)] * 3,
        compiler_params=pltpu.CompilerParams(vmem_limit_bytes=24 * 1024 * 1024),
        cost_estimate=pl.CostEstimate(flops=10350000000, bytes_accessed=32400000, transcendentals=0),
        name="attention",
    )(xi, units, qkv, *hs)


def pack_kernel(q, k, v, out):
    for i in range(16):
        cols = pl.ds(i * HEAD, HEAD)
        out[i, 0] = q[:, cols]
        out[i, 1] = k[:, cols]
        out[i, 2] = v[:, cols]


def pack(q, k, v):
    vm = pl.BlockSpec(memory_space=pltpu.VMEM)
    return pl.pallas_call(
        pack_kernel,
        out_shape=jax.ShapeDtypeStruct((16, 3, TOK, HEAD), BF),
        in_specs=[vm] * 3,
        out_specs=vm,
        cost_estimate=pl.CostEstimate(flops=1150000, bytes_accessed=3600, transcendentals=0),
        name="pack",
    )(q, k, v)


def unpack_kernel(grads, q, k, v):
    for i in range(16):
        cols = pl.ds(i * HEAD, HEAD)
        q[:, cols] = grads[i, 0]
        k[:, cols] = grads[i, 1]
        v[:, cols] = grads[i, 2]


def unpack(grads):
    rows = TOK // 2
    return pl.pallas_call(
        unpack_kernel,
        grid=(2,),
        out_shape=[jax.ShapeDtypeStruct((TOK, 16 * HEAD), BF)] * 3,
        in_specs=[pl.BlockSpec((16, 3, rows, HEAD), lambda i: (0, 0, i, 0))],
        out_specs=[pl.BlockSpec((rows, 16 * HEAD), lambda i: (i, 0))] * 3,
        compiler_params=pltpu.CompilerParams(vmem_limit_bytes=63 * 1024 * 1024),
        cost_estimate=pl.CostEstimate(flops=1, bytes_accessed=1, transcendentals=0),
        name="unpack",
    )(grads)


def three_terms(value):
    high = value.astype(BF)
    rest = value - high.astype(F32)
    middle = rest.astype(BF)
    return jnp.concatenate([high, middle, (rest - middle.astype(F32)).astype(BF), jnp.zeros_like(high)], axis=0)


def pack_out_kernel(o, out):
    for y in range(4):
        for x in range(4):
            out[y, :, pl.ds(x * HEAD, HEAD)] = o[:, pl.ds((4 * x + y) * HEAD, HEAD)]


def pack_out(o):
    vm = pl.BlockSpec(memory_space=pltpu.VMEM)
    return pl.pallas_call(
        pack_out_kernel,
        out_shape=jax.ShapeDtypeStruct((4, TOK, 4 * HEAD), BF),
        in_specs=[vm],
        out_specs=vm,
        cost_estimate=pl.CostEstimate(flops=1, bytes_accessed=1, transcendentals=0),
        name="pack_out",
    )(o)


def chunk_copies(pieces, whole, sems, c):
    cols = pl.ds(c * CHUNK, CHUNK)
    copies = []
    for n, (ref, row) in enumerate(pieces):
        rows = ref.shape[0]
        copies.append(
            pltpu.make_async_copy(
                ref.at[:, cols], whole.at[pl.ds(pl.multiple_of(row, 64), rows), cols], sems.at[c, n]
            )
        )
    return copies


def grad_pieces(y, g, back, ahead, fa, fb):
    far = lax.rem(y + 2, 4) * TOK
    return [(g, y * TOK), (back, lax.rem(y + 3, 4) * TOK), (ahead, lax.rem(y + 1, 4) * TOK), (fa, far), (fb, far + 64)]


def block_kernel(at, *refs):
    g, (w, wa, wb, wc, wd, o), (mine, *other), hs = refs[:5], refs[5:11], refs[11:14], refs[14:18]
    gs, ws, term, staged, acc, gsem, wsem, osem = refs[18:]
    x, y, core = at[0], at[1], at[2]
    g_pieces = grad_pieces(y, *g)
    near = lax.select(core == 0, 1, 3)
    w_pieces = [
        (w, 0),
        (wa, near * TOK),
        (wb, (4 - near) * TOK),
        (wc, 2 * TOK + 64 * core),
        (wd, 2 * TOK + 64 * (1 - core)),
    ]
    g_copies = [chunk_copies(g_pieces, gs, gsem, c) for c in range(MODEL // CHUNK)]
    w_copies = [chunk_copies(w_pieces, ws, wsem, c) for c in range(MODEL // CHUNK)]
    for pair in zip(g_copies, w_copies):
        for copy in pair[0] + pair[1]:
            copy.start()
    outs = o[...].reshape(4 * TOK, 4 * HEAD)
    for c in range(MODEL // CHUNK):
        cols = pl.ds(c * CHUNK, CHUNK)
        for copy in g_copies[c]:
            copy.wait()
        term[cols, :] = tn(gs[:, cols], outs)
        for m in range(CHUNK * c // 200, CHUNK * (c + 1) // 200):
            staged[m] = term[pl.ds(200 * m, 200), :].astype(BF)
            z = m // 2
            inside = staged.at[m], mine.at[z], osem.at[m]
            outside = staged.at[m], other[z // 4].at[z % 4], osem.at[m]
            pl.when(core == m % 2)(lambda refs=inside: pltpu.make_async_copy(*refs).start())
            pl.when(core != m % 2)(lambda refs=outside: pltpu.make_async_copy(*refs).start())
        for copy in w_copies[c]:
            copy.wait()
        part = nt(gs[:, cols], ws[:, cols])
        if c == 0:
            acc[...] = part
        else:
            acc[...] += part
    for k in range(4):
        own = pl.ds(pl.multiple_of(lax.rem(x + 4 - k, 4) * HEAD, HEAD), HEAD)
        lines = []
        for j in range(4):
            rows = pl.ds(j * TOK, TOK)
            h = acc[rows, pl.ds(k * HEAD, HEAD)].astype(BF)
            hs[k][rows, :] = h
            product = h.astype(F32) * o[j, :, own].astype(F32)
            lines.append(jnp.sum(product.T, axis=0, keepdims=True))
        hs[k][pl.ds(4 * TOK, 16), :] = three_terms(jnp.concatenate(lines, axis=0))
    for m in range(16):
        pltpu.make_async_copy(staged.at[m], mine.at[m // 2], osem.at[m]).wait()


def blocks(at, g, w, o):
    vm = pl.BlockSpec(memory_space=pltpu.VMEM)
    sm = pl.BlockSpec(memory_space=pltpu.SMEM)
    hbm = pl.BlockSpec(memory_space=pl.ANY)
    sizes = [(n, 200, 4 * HEAD) for n in (8, 4, 4)] + [(4 * TOK + 16, HEAD)] * 4
    return pl.pallas_call(
        block_kernel,
        out_shape=[jax.ShapeDtypeStruct(size, BF) for size in sizes],
        in_specs=[sm] + [hbm] * 10 + [vm],
        out_specs=[hbm] * 3 + [vm] * 4,
        scratch_shapes=[
            pltpu.VMEM((4 * TOK, MODEL), BF),
            pltpu.VMEM((4 * HEAD, MODEL), BF),
            pltpu.VMEM((MODEL, 4 * HEAD), F32),
            pltpu.VMEM((16, 200, 4 * HEAD), BF),
            pltpu.VMEM((4 * TOK, 4 * HEAD), F32),
            pltpu.SemaphoreType.DMA((MODEL // CHUNK, 5)),
            pltpu.SemaphoreType.DMA((MODEL // CHUNK, 5)),
            pltpu.SemaphoreType.DMA((16,)),
        ],
        compiler_params=pltpu.CompilerParams(vmem_limit_bytes=60 * 1024 * 1024),
        cost_estimate=pl.CostEstimate(flops=10350000000, bytes_accessed=32400000, transcendentals=0),
        name="blocks",
    )(at, *g, *w, o)


def pair_kernel(ks, at, mine, *refs):
    other, outs = refs[:2], refs[2:]
    for n, k in enumerate(ks):
        cols = pl.ds(pl.multiple_of(lax.rem(at[0] + k, 4) * HEAD, HEAD), HEAD)
        for z in range(8):
            outs[n][z] = (mine[z, :, cols].astype(F32) + other[z // 4][z % 4, :, cols].astype(F32)).astype(BF)


def pair_sum(ks, at, mine, *other):
    vm = pl.BlockSpec(memory_space=pltpu.VMEM)
    sm = pl.BlockSpec(memory_space=pltpu.SMEM)
    return pl.pallas_call(
        lambda *refs: pair_kernel(ks, *refs),
        out_shape=[jax.ShapeDtypeStruct((8, 200, HEAD), BF)] * len(ks),
        in_specs=[sm] + [vm] * 3,
        out_specs=[vm] * len(ks),
        cost_estimate=pl.CostEstimate(flops=1, bytes_accessed=1, transcendentals=0),
        name=f"pair_sum_{len(ks)}",
    )(at, mine, *other)


def on_device(queries, keys_in, values_in, saved_out, out_grad, out_weight, image_units):
    seq = lax.axis_index("seq").astype(jnp.int32)
    dp = lax.axis_index("dp").astype(jnp.int32)
    core, z = lax.rem(dp, 2), lax.div(dp, 2)
    at = jnp.stack([lax.div(seq, 4), lax.rem(seq, 4), core, z])
    after = lax.optimization_barrier
    move = lax.ppermute

    g = out_grad[0]
    back, ahead = move(g, "seq", YS[1]), move(g, "seq", YS[3])
    wa = move(out_weight, ("dp", "seq"), BOTH)
    wc = move(lax.dynamic_slice_in_dim(out_weight, 64 * core, 64, 0), "seq", XS[2])
    o_rows = lax.all_to_all(
        pack_out(saved_out[0]), "seq", split_axis=0, concat_axis=0, tiled=True, axis_index_groups=YGROUPS
    )
    back, ahead, wa, wc, o_rows, at = after((back, ahead, wa, wc, o_rows, at))
    q, fa, fb = after((queries[0], back[:64], ahead[64:]))
    fa, fb = move(fa, "seq", YS[1]), move(fb, "seq", YS[3])
    wb, wd = move(wa, "dp", CORES), move(wc, "dp", CORES)
    qkv = lax.all_to_all(pack(q, keys_in[0], values_in[0]), "seq", split_axis=0, concat_axis=0, tiled=True)
    g_pieces = (g, back, ahead, fa, fb)

    mine, *other, h0, h1, h2, h3 = blocks(at, g_pieces, (out_weight, wa, wb, wc, wd), o_rows)
    heads = [h0] + [move(h, "seq", XS[4 - k]) for k, h in ((1, h1), (2, h2), (3, h3))]

    other = [move(part, "dp", CORES) for part in other]
    pairs = pair_sum((1, 2, 3), at, mine, *other)
    qkv, *_ = after((qkv, *pairs))
    grads = attention(at, image_units[0], qkv, heads)
    grads, mine, *other = after((grads, mine, *other))
    sent = lax.all_to_all(grads, "seq", split_axis=0, concat_axis=0, tiled=True)
    query_grad, key_grad, value_grad = unpack(sent)

    total = pair_sum((0,), at, mine, *other)[0].astype(F32)
    for k in (1, 2, 3):
        total = total + move(pairs[k - 1], "seq", XS[k]).astype(F32)
    total = total.reshape(4, 2, 200, HEAD)
    bit, quarter = lax.rem(z, 2), lax.div(z, 2)
    away = lax.dynamic_index_in_dim(total, 1 - bit, 1, keepdims=False).astype(BF)
    total = lax.dynamic_index_in_dim(total, bit, 1, keepdims=False) + move(away, "dp", ZNEAR).astype(F32)
    parts = [lax.dynamic_index_in_dim(total, quarter, 0, keepdims=False)]
    for k in (1, 2, 3):
        part = lax.dynamic_index_in_dim(total, lax.rem(quarter + k, 4), 0, keepdims=False).astype(BF)
        parts.append(move(part, "dp", ZFAR[k]))
    *parts, query_grad, key_grad, value_grad = after((*parts, query_grad, key_grad, value_grad))
    last = sum([part.astype(F32) for part in parts[1:]], parts[0])
    weight_grad = last.T * (1.0 / math.sqrt(PACK * 16))
    return query_grad[None], key_grad[None], value_grad[None], weight_grad


def solution(mesh):
    rows = P("dp", "seq", None)
    return jax.shard_map(
        on_device,
        mesh=mesh,
        in_specs=(rows, rows, rows, rows, rows, P("seq", None), P("dp", None)),
        out_specs=(rows, rows, rows, P("seq", "dp")),
        check_vma=False,
    )
```

```python
import math

import jax
import jax.numpy as jnp
from jax import lax
from jax.experimental import pallas as pl
from jax.experimental.pallas import tpu as pltpu
from jax.sharding import PartitionSpec as P

HEAD = 128
PACK = 2048
TOK = 128
MODEL = 3200
IMG = 512
SEGS = 8
NEG = -1e30
BF = jnp.bfloat16
F32 = jnp.float32
XS = [[(4 * x + y, 4 * ((x + k) % 4) + y) for x in range(4) for y in range(4)] for k in range(4)]
YS = [[(4 * x + y, 4 * x + (y + k) % 4) for x in range(4) for y in range(4)] for k in range(4)]
YGROUPS = [[4 * x + y for y in range(4)] for x in range(4)]
CORES = [(i, i ^ 1) for i in range(16)]
ZNEAR = [(2 * z + c, 2 * (z ^ 1) + c) for z in range(8) for c in range(2)]
ZFAR = [[(2 * z + c, 2 * ((z + 2 * k) % 8) + c) for z in range(8) for c in range(2)] for k in range(4)]
BOTH = [
    (16 * d + 4 * x + y, 16 * d + 4 * ((x + (1, 3)[d % 2]) % 4) + y)
    for d in range(16)
    for x in range(4)
    for y in range(4)
]
CHUNK = 640


def nt(a, b):
    return lax.dot_general(a, b, (((1,), (1,)), ((), ())), preferred_element_type=F32)


def nn(a, b):
    return lax.dot_general(a, b, (((1,), (0,)), ((), ())), preferred_element_type=F32)


def tn(a, b):
    return lax.dot_general(a, b, (((0,), (0,)), ((), ())), preferred_element_type=F32)


def attention_kernel(xi, units, qkv, h0, h1, h2, h3, out, qs, ks, vs, hs, ds_, gq, gk, gv):
    for i in range(16):
        rows = pl.ds(i * TOK, TOK)
        qs[rows, :] = qkv[i, 0]
        ks[rows, :] = qkv[i, 1]
        vs[rows, :] = qkv[i, 2]
    tail = pl.ds(PACK, IMG)
    for ref in (qs, ks, vs, hs):
        ref[tail, :] = jnp.zeros((IMG, HEAD), BF)
    ds_[pl.ds(16, 8), :] = jnp.zeros((8, HEAD), F32)
    for k, h in enumerate((h0, h1, h2, h3)):
        block = lax.rem(xi[0] + k, 4)
        hs[pl.ds(pl.multiple_of(block * IMG, IMG), IMG), :] = h[pl.ds(0, IMG), :]
        parts = h[pl.ds(IMG, 16), :].astype(F32)
        ds_[pl.ds(block * 4, 4), :] = parts[0:4] + parts[4:8] + parts[8:12]
    scaling = 1.0 / math.sqrt(HEAD)
    to_two = scaling * math.log2(math.e)

    def image(start, size, width, step):
        kw = ks[pl.ds(start, width), :]
        vw = vs[pl.ds(start, width), :]
        row = lax.broadcasted_iota(jnp.int32, (width, 1), 0)
        bias = jnp.where(row < size, 0.0, NEG).astype(F32)
        first = lax.div(start, TOK)
        shift = start - first * TOK
        gk_sum = gv_sum = None
        for b in range(width // step):
            here = pl.ds(pl.multiple_of(start + b * step, 16), step)
            qb = qs[here, :]
            hb = hs[here, :]
            lane = lax.broadcasted_iota(jnp.int32, (1, step), 1) + b * step
            pieces = []
            for n in range(step // TOK):
                line = first + b * (step // TOK) + n
                two = jnp.concatenate([ds_[pl.ds(line, 1), :], ds_[pl.ds(line + 1, 1), :]], axis=1)
                pieces.append(pltpu.roll(two, 2 * TOK - shift, 1)[:, :TOK])
            delta = pieces[0] if len(pieces) == 1 else jnp.concatenate(pieces, axis=1)
            s = nt(kw, qb) * to_two + bias
            top = jnp.max(s, axis=0, keepdims=True)
            e = jnp.exp2(s - top)
            norm = jnp.where(lane < size, 1.0 / jnp.sum(e, axis=0, keepdims=True), 0.0)
            p = e * norm
            dp = nt(vw, hb)
            dsc = (p * (dp - delta)).astype(BF)
            pk = nn(dsc, qb)
            pv = nn(p.astype(BF), hb)
            gk_sum = pk if gk_sum is None else gk_sum + pk
            gv_sum = pv if gv_sum is None else gv_sum + pv
            gq[here, :] = (tn(dsc, kw) * scaling).astype(BF)
        gk[pl.ds(start, width), :] = (gk_sum * scaling).astype(BF)
        gv[pl.ds(start, width), :] = gv_sum.astype(BF)

    def one(j, start):
        size = units[j] * 16
        start = pl.multiple_of(start, 16)
        for width, step in ((128, 128), (256, 256), (384, 384), (512, 512)):
            pl.when((size > width - 128) & (size <= width))(lambda width=width, step=step: image(start, size, width, step))
        return start + size

    lax.fori_loop(0, SEGS, one, jnp.int32(0))
    for i in range(16):
        rows = pl.ds(i * TOK, TOK)
        out[i, 0] = gq[rows, :]
        out[i, 1] = gk[rows, :]
        out[i, 2] = gv[rows, :]


def attention(xi, units, qkv, hs):
    vm = pl.BlockSpec(memory_space=pltpu.VMEM)
    sm = pl.BlockSpec(memory_space=pltpu.SMEM)
    return pl.pallas_call(
        attention_kernel,
        out_shape=jax.ShapeDtypeStruct((16, 3, TOK, HEAD), BF),
        in_specs=[sm, sm] + [vm] * 5,
        out_specs=vm,
        scratch_shapes=[pltpu.VMEM((PACK + IMG, HEAD), BF)] * 4 + [pltpu.VMEM((24, HEAD), F32)] + [pltpu.VMEM((PACK + IMG, HEAD), BF)] * 3,
        compiler_params=pltpu.CompilerParams(vmem_limit_bytes=24 * 1024 * 1024),
        cost_estimate=pl.CostEstimate(flops=10350000000, bytes_accessed=32400000, transcendentals=0),
        name="attention",
    )(xi, units, qkv, *hs)


def pack_kernel(q, k, v, out):
    for i in range(16):
        cols = pl.ds(i * HEAD, HEAD)
        out[i, 0] = q[:, cols]
        out[i, 1] = k[:, cols]
        out[i, 2] = v[:, cols]


def pack(q, k, v):
    vm = pl.BlockSpec(memory_space=pltpu.VMEM)
    return pl.pallas_call(
        pack_kernel,
        out_shape=jax.ShapeDtypeStruct((16, 3, TOK, HEAD), BF),
        in_specs=[vm] * 3,
        out_specs=vm,
        cost_estimate=pl.CostEstimate(flops=1150000, bytes_accessed=3600, transcendentals=0),
        name="pack",
    )(q, k, v)


def unpack_kernel(grads, own, a, b, c, q, k, v, weight):
    for i in range(16):
        cols = pl.ds(i * HEAD, HEAD)
        q[:, cols] = grads[i, 0]
        k[:, cols] = grads[i, 1]
        v[:, cols] = grads[i, 2]
    total = own[...] + a[...].astype(F32) + b[...].astype(F32) + c[...].astype(F32)
    weight[...] = total * (1.0 / math.sqrt(PACK * 16))


def unpack(grads, parts):
    rows = TOK // 2
    whole = pl.BlockSpec((200, HEAD), lambda i: (0, 0))
    return pl.pallas_call(
        unpack_kernel,
        grid=(2,),
        out_shape=[jax.ShapeDtypeStruct((TOK, 16 * HEAD), BF)] * 3 + [jax.ShapeDtypeStruct((200, HEAD), F32)],
        in_specs=[pl.BlockSpec((16, 3, rows, HEAD), lambda i: (0, 0, i, 0))] + [whole] * 4,
        out_specs=[pl.BlockSpec((rows, 16 * HEAD), lambda i: (i, 0))] * 3 + [whole],
        compiler_params=pltpu.CompilerParams(vmem_limit_bytes=63 * 1024 * 1024),
        cost_estimate=pl.CostEstimate(flops=1, bytes_accessed=1, transcendentals=0),
        name="unpack",
    )(grads, *parts)


def three_terms(value):
    high = value.astype(BF)
    rest = value - high.astype(F32)
    middle = rest.astype(BF)
    return jnp.concatenate([high, middle, (rest - middle.astype(F32)).astype(BF), jnp.zeros_like(high)], axis=0)


def pack_out_kernel(o, out):
    for y in range(4):
        for x in range(4):
            out[y, :, pl.ds(x * HEAD, HEAD)] = o[:, pl.ds((4 * x + y) * HEAD, HEAD)]


def pack_out(o):
    vm = pl.BlockSpec(memory_space=pltpu.VMEM)
    return pl.pallas_call(
        pack_out_kernel,
        out_shape=jax.ShapeDtypeStruct((4, TOK, 4 * HEAD), BF),
        in_specs=[vm],
        out_specs=vm,
        cost_estimate=pl.CostEstimate(flops=1, bytes_accessed=1, transcendentals=0),
        name="pack_out",
    )(o)


def chunk_copies(pieces, whole, sems, c):
    cols = pl.ds(c * CHUNK, CHUNK)
    copies = []
    for n, (ref, row) in enumerate(pieces):
        rows = ref.shape[0]
        copies.append(
            pltpu.make_async_copy(
                ref.at[:, cols], whole.at[pl.ds(pl.multiple_of(row, 64), rows), cols], sems.at[c, n]
            )
        )
    return copies


def grad_pieces(y, g, back, ahead, fa, fb):
    far = lax.rem(y + 2, 4) * TOK
    return [(g, y * TOK), (back, lax.rem(y + 3, 4) * TOK), (ahead, lax.rem(y + 1, 4) * TOK), (fa, far), (fb, far + 64)]


def block_kernel(at, *refs):
    g, (w, wa, wb, wc, wd, o), (mine, *other), hs = refs[:5], refs[5:11], refs[11:14], refs[14:18]
    gs, ws, term, staged, acc, gsem, wsem, osem = refs[18:]
    x, y, core = at[0], at[1], at[2]
    g_pieces = grad_pieces(y, *g)
    near = lax.select(core == 0, 1, 3)
    w_pieces = [
        (w, 0),
        (wa, near * TOK),
        (wb, (4 - near) * TOK),
        (wc, 2 * TOK + 64 * core),
        (wd, 2 * TOK + 64 * (1 - core)),
    ]
    g_copies = [chunk_copies(g_pieces, gs, gsem, c) for c in range(MODEL // CHUNK)]
    w_copies = [chunk_copies(w_pieces, ws, wsem, c) for c in range(MODEL // CHUNK)]
    for pair in zip(g_copies, w_copies):
        for copy in pair[0] + pair[1]:
            copy.start()
    outs = o[...].reshape(4 * TOK, 4 * HEAD)
    for c in range(MODEL // CHUNK):
        cols = pl.ds(c * CHUNK, CHUNK)
        for copy in g_copies[c]:
            copy.wait()
        term[cols, :] = tn(gs[:, cols], outs)
        for m in range(CHUNK * c // 200, CHUNK * (c + 1) // 200):
            staged[m] = term[pl.ds(200 * m, 200), :].astype(BF)
            z = m // 2
            inside = staged.at[m], mine.at[z], osem.at[m]
            outside = staged.at[m], other[z // 4].at[z % 4], osem.at[m]
            pl.when(core == m % 2)(lambda refs=inside: pltpu.make_async_copy(*refs).start())
            pl.when(core != m % 2)(lambda refs=outside: pltpu.make_async_copy(*refs).start())
        for copy in w_copies[c]:
            copy.wait()
        part = nt(gs[:, cols], ws[:, cols])
        if c == 0:
            acc[...] = part
        else:
            acc[...] += part
    for k in range(4):
        own = pl.ds(pl.multiple_of(lax.rem(x + 4 - k, 4) * HEAD, HEAD), HEAD)
        lines = []
        for j in range(4):
            rows = pl.ds(j * TOK, TOK)
            h = acc[rows, pl.ds(k * HEAD, HEAD)].astype(BF)
            hs[k][rows, :] = h
            product = h.astype(F32) * o[j, :, own].astype(F32)
            lines.append(jnp.sum(product.T, axis=0, keepdims=True))
        hs[k][pl.ds(4 * TOK, 16), :] = three_terms(jnp.concatenate(lines, axis=0))
    for m in range(16):
        pltpu.make_async_copy(staged.at[m], mine.at[m // 2], osem.at[m]).wait()


def blocks(at, g, w, o):
    vm = pl.BlockSpec(memory_space=pltpu.VMEM)
    sm = pl.BlockSpec(memory_space=pltpu.SMEM)
    hbm = pl.BlockSpec(memory_space=pl.ANY)
    sizes = [(n, 200, 4 * HEAD) for n in (8, 4, 4)] + [(4 * TOK + 16, HEAD)] * 4
    return pl.pallas_call(
        block_kernel,
        out_shape=[jax.ShapeDtypeStruct(size, BF) for size in sizes],
        in_specs=[sm] + [hbm] * 10 + [vm],
        out_specs=[hbm] * 3 + [vm] * 4,
        scratch_shapes=[
            pltpu.VMEM((4 * TOK, MODEL), BF),
            pltpu.VMEM((4 * HEAD, MODEL), BF),
            pltpu.VMEM((MODEL, 4 * HEAD), F32),
            pltpu.VMEM((16, 200, 4 * HEAD), BF),
            pltpu.VMEM((4 * TOK, 4 * HEAD), F32),
            pltpu.SemaphoreType.DMA((MODEL // CHUNK, 5)),
            pltpu.SemaphoreType.DMA((MODEL // CHUNK, 5)),
            pltpu.SemaphoreType.DMA((16,)),
        ],
        compiler_params=pltpu.CompilerParams(vmem_limit_bytes=60 * 1024 * 1024),
        cost_estimate=pl.CostEstimate(flops=10350000000, bytes_accessed=32400000, transcendentals=0),
        name="blocks",
    )(at, *g, *w, o)


def pair_kernel(at, mine, *refs):
    other, outs = refs[:2], refs[2:]
    for k in range(4):
        cols = pl.ds(pl.multiple_of(lax.rem(at[0] + k, 4) * HEAD, HEAD), HEAD)
        for z in range(8):
            outs[k][z] = (mine[z, :, cols].astype(F32) + other[z // 4][z % 4, :, cols].astype(F32)).astype(BF)


def pair_sum(at, mine, *other):
    vm = pl.BlockSpec(memory_space=pltpu.VMEM)
    sm = pl.BlockSpec(memory_space=pltpu.SMEM)
    return pl.pallas_call(
        pair_kernel,
        out_shape=[jax.ShapeDtypeStruct((8, 200, HEAD), BF)] * 4,
        in_specs=[sm] + [vm] * 3,
        out_specs=[vm] * 4,
        cost_estimate=pl.CostEstimate(flops=1, bytes_accessed=1, transcendentals=0),
        name="pair_sum",
    )(at, mine, *other)


def on_device(queries, keys_in, values_in, saved_out, out_grad, out_weight, image_units):
    seq = lax.axis_index("seq").astype(jnp.int32)
    dp = lax.axis_index("dp").astype(jnp.int32)
    core, z = lax.rem(dp, 2), lax.div(dp, 2)
    at = jnp.stack([lax.div(seq, 4), lax.rem(seq, 4), core, z])
    after = lax.optimization_barrier
    move = lax.ppermute

    g = out_grad[0]
    back, ahead = move(g, "seq", YS[1]), move(g, "seq", YS[3])
    wa = move(out_weight, ("dp", "seq"), BOTH)
    wc = move(lax.dynamic_slice_in_dim(out_weight, 64 * core, 64, 0), "seq", XS[2])
    o_rows = lax.all_to_all(
        pack_out(saved_out[0]), "seq", split_axis=0, concat_axis=0, tiled=True, axis_index_groups=YGROUPS
    )
    back, ahead, wa, wc, o_rows, at = after((back, ahead, wa, wc, o_rows, at))
    q, fa, fb = after((queries[0], back[:64], ahead[64:]))
    fa, fb = move(fa, "seq", YS[1]), move(fb, "seq", YS[3])
    wb, wd = move(wa, "dp", CORES), move(wc, "dp", CORES)
    qkv = lax.all_to_all(pack(q, keys_in[0], values_in[0]), "seq", split_axis=0, concat_axis=0, tiled=True)
    g_pieces = (g, back, ahead, fa, fb)

    mine, *other, h0, h1, h2, h3 = blocks(at, g_pieces, (out_weight, wa, wb, wc, wd), o_rows)
    heads = [h0] + [move(h, "seq", XS[4 - k]) for k, h in ((1, h1), (2, h2), (3, h3))]

    pairs = pair_sum(at, mine, *[move(part, "dp", CORES) for part in other])
    qkv, *_ = after((qkv, *pairs))
    grads = attention(at, image_units[0], qkv, heads)
    sent = lax.all_to_all(grads, "seq", split_axis=0, concat_axis=0, tiled=True)

    total = pairs[0].astype(F32)
    for k in (1, 2, 3):
        total = total + move(pairs[k], "seq", XS[k]).astype(F32)
    total = total.reshape(4, 2, 200, HEAD)
    bit, quarter = lax.rem(z, 2), lax.div(z, 2)
    away = lax.dynamic_index_in_dim(total, 1 - bit, 1, keepdims=False).astype(BF)
    total = lax.dynamic_index_in_dim(total, bit, 1, keepdims=False) + move(away, "dp", ZNEAR).astype(F32)
    parts = [lax.dynamic_index_in_dim(total, quarter, 0, keepdims=False)]
    for k in (1, 2, 3):
        part = lax.dynamic_index_in_dim(total, lax.rem(quarter + k, 4), 0, keepdims=False).astype(BF)
        parts.append(move(part, "dp", ZFAR[k]))
    query_grad, key_grad, value_grad, weight = unpack(sent, parts)
    return query_grad[None], key_grad[None], value_grad[None], weight.T


def solution(mesh):
    rows = P("dp", "seq", None)
    return jax.shard_map(
        on_device,
        mesh=mesh,
        in_specs=(rows, rows, rows, rows, rows, P("seq", None), P("dp", None)),
        out_specs=(rows, rows, rows, P("seq", "dp")),
        check_vma=False,
    )
```

```python
import math

import jax
import jax.numpy as jnp
from jax import lax
from jax.experimental import pallas as pl
from jax.experimental.pallas import tpu as pltpu
from jax.sharding import PartitionSpec as P

HEAD = 128
PACK = 2048
TOK = 128
MODEL = 3200
IMG = 512
SEGS = 8
NEG = -1e30
BF = jnp.bfloat16
F32 = jnp.float32
XS = [[(4 * x + y, 4 * ((x + k) % 4) + y) for x in range(4) for y in range(4)] for k in range(4)]
YS = [[(4 * x + y, 4 * x + (y + k) % 4) for x in range(4) for y in range(4)] for k in range(4)]
YGROUPS = [[4 * x + y for y in range(4)] for x in range(4)]
CORES = [(i, i ^ 1) for i in range(16)]
ZNEAR = [(2 * z + c, 2 * (z ^ 1) + c) for z in range(8) for c in range(2)]
ZFAR = [[(2 * z + c, 2 * ((z + 2 * k) % 8) + c) for z in range(8) for c in range(2)] for k in range(4)]
BOTH = [
    (16 * d + 4 * x + y, 16 * d + 4 * ((x + (1, 3)[d % 2]) % 4) + y)
    for d in range(16)
    for x in range(4)
    for y in range(4)
]
CHUNK = 640


def nt(a, b):
    return lax.dot_general(a, b, (((1,), (1,)), ((), ())), preferred_element_type=F32)


def nn(a, b):
    return lax.dot_general(a, b, (((1,), (0,)), ((), ())), preferred_element_type=F32)


def tn(a, b):
    return lax.dot_general(a, b, (((0,), (0,)), ((), ())), preferred_element_type=F32)


def attention_kernel(xi, units, qkv, h0, h1, h2, h3, out, qs, ks, vs, hs, ds_, gq, gk, gv):
    for i in range(16):
        rows = pl.ds(i * TOK, TOK)
        qs[rows, :] = qkv[i, 0]
        ks[rows, :] = qkv[i, 1]
        vs[rows, :] = qkv[i, 2]
    tail = pl.ds(PACK, IMG)
    for ref in (qs, ks, vs, hs):
        ref[tail, :] = jnp.zeros((IMG, HEAD), BF)
    ds_[pl.ds(16, 8), :] = jnp.zeros((8, HEAD), F32)
    for k, h in enumerate((h0, h1, h2, h3)):
        block = lax.rem(xi[0] + k, 4)
        hs[pl.ds(pl.multiple_of(block * IMG, IMG), IMG), :] = h[pl.ds(0, IMG), :]
        parts = h[pl.ds(IMG, 16), :].astype(F32)
        ds_[pl.ds(block * 4, 4), :] = parts[0:4] + parts[4:8] + parts[8:12]
    scaling = 1.0 / math.sqrt(HEAD)
    to_two = scaling * math.log2(math.e)

    def image(start, size, width, step):
        kw = ks[pl.ds(start, width), :]
        vw = vs[pl.ds(start, width), :]
        row = lax.broadcasted_iota(jnp.int32, (width, 1), 0)
        bias = jnp.where(row < size, 0.0, NEG).astype(F32)
        first = lax.div(start, TOK)
        shift = start - first * TOK
        gk_sum = gv_sum = None
        for b in range(width // step):
            here = pl.ds(pl.multiple_of(start + b * step, 16), step)
            qb = qs[here, :]
            hb = hs[here, :]
            lane = lax.broadcasted_iota(jnp.int32, (1, step), 1) + b * step
            pieces = []
            for n in range(step // TOK):
                line = first + b * (step // TOK) + n
                two = jnp.concatenate([ds_[pl.ds(line, 1), :], ds_[pl.ds(line + 1, 1), :]], axis=1)
                pieces.append(pltpu.roll(two, 2 * TOK - shift, 1)[:, :TOK])
            delta = pieces[0] if len(pieces) == 1 else jnp.concatenate(pieces, axis=1)
            s = nt(kw, qb) * to_two + bias
            top = jnp.max(s, axis=0, keepdims=True)
            e = jnp.exp2(s - top)
            norm = jnp.where(lane < size, 1.0 / jnp.sum(e, axis=0, keepdims=True), 0.0)
            p = e * norm
            dp = nt(vw, hb)
            dsc = (p * (dp - delta)).astype(BF)
            pk = nn(dsc, qb)
            pv = nn(p.astype(BF), hb)
            gk_sum = pk if gk_sum is None else gk_sum + pk
            gv_sum = pv if gv_sum is None else gv_sum + pv
            gq[here, :] = (tn(dsc, kw) * scaling).astype(BF)
        gk[pl.ds(start, width), :] = (gk_sum * scaling).astype(BF)
        gv[pl.ds(start, width), :] = gv_sum.astype(BF)

    def one(j, start):
        size = units[j] * 16
        start = pl.multiple_of(start, 16)
        for width, step in ((128, 128), (256, 256), (384, 384), (512, 512)):
            pl.when((size > width - 128) & (size <= width))(lambda width=width, step=step: image(start, size, width, step))
        return start + size

    lax.fori_loop(0, SEGS, one, jnp.int32(0))
    for i in range(16):
        rows = pl.ds(i * TOK, TOK)
        out[i, 0] = gq[rows, :]
        out[i, 1] = gk[rows, :]
        out[i, 2] = gv[rows, :]


def attention(xi, units, qkv, hs):
    vm = pl.BlockSpec(memory_space=pltpu.VMEM)
    sm = pl.BlockSpec(memory_space=pltpu.SMEM)
    return pl.pallas_call(
        attention_kernel,
        out_shape=jax.ShapeDtypeStruct((16, 3, TOK, HEAD), BF),
        in_specs=[sm, sm] + [vm] * 5,
        out_specs=vm,
        scratch_shapes=[pltpu.VMEM((PACK + IMG, HEAD), BF)] * 4 + [pltpu.VMEM((24, HEAD), F32)] + [pltpu.VMEM((PACK + IMG, HEAD), BF)] * 3,
        compiler_params=pltpu.CompilerParams(vmem_limit_bytes=24 * 1024 * 1024),
        cost_estimate=pl.CostEstimate(flops=10350000000, bytes_accessed=32400000, transcendentals=0),
        name="attention",
    )(xi, units, qkv, *hs)


def pack_kernel(q, k, v, out):
    for i in range(16):
        cols = pl.ds(i * HEAD, HEAD)
        out[i, 0] = q[:, cols]
        out[i, 1] = k[:, cols]
        out[i, 2] = v[:, cols]


def pack(q, k, v):
    rows = TOK // 2
    return pl.pallas_call(
        pack_kernel,
        grid=(2,),
        out_shape=jax.ShapeDtypeStruct((16, 3, TOK, HEAD), BF),
        in_specs=[pl.BlockSpec((rows, 16 * HEAD), lambda i: (i, 0))] * 3,
        out_specs=pl.BlockSpec((16, 3, rows, HEAD), lambda i: (0, 0, i, 0)),
        cost_estimate=pl.CostEstimate(flops=1, bytes_accessed=1, transcendentals=0),
        name="pack",
    )(q, k, v)


def unpack_kernel(grads, q, k, v):
    for i in range(16):
        cols = pl.ds(i * HEAD, HEAD)
        q[:, cols] = grads[i, 0]
        k[:, cols] = grads[i, 1]
        v[:, cols] = grads[i, 2]


def unpack(grads):
    rows = TOK // 2
    return pl.pallas_call(
        unpack_kernel,
        grid=(2,),
        out_shape=[jax.ShapeDtypeStruct((TOK, 16 * HEAD), BF)] * 3,
        in_specs=[pl.BlockSpec((16, 3, rows, HEAD), lambda i: (0, 0, i, 0))],
        out_specs=[pl.BlockSpec((rows, 16 * HEAD), lambda i: (i, 0))] * 3,
        compiler_params=pltpu.CompilerParams(vmem_limit_bytes=63 * 1024 * 1024),
        cost_estimate=pl.CostEstimate(flops=1, bytes_accessed=1, transcendentals=0),
        name="unpack",
    )(grads)


def three_terms(value):
    high = value.astype(BF)
    rest = value - high.astype(F32)
    middle = rest.astype(BF)
    return jnp.concatenate([high, middle, (rest - middle.astype(F32)).astype(BF), jnp.zeros_like(high)], axis=0)


def pack_out_kernel(o, out):
    for y in range(4):
        for x in range(4):
            out[y, :, pl.ds(x * HEAD, HEAD)] = o[:, pl.ds((4 * x + y) * HEAD, HEAD)]


def pack_out(o):
    vm = pl.BlockSpec(memory_space=pltpu.VMEM)
    return pl.pallas_call(
        pack_out_kernel,
        out_shape=jax.ShapeDtypeStruct((4, TOK, 4 * HEAD), BF),
        in_specs=[vm],
        out_specs=vm,
        cost_estimate=pl.CostEstimate(flops=1, bytes_accessed=1, transcendentals=0),
        name="pack_out",
    )(o)


def chunk_copies(pieces, whole, sems, c):
    cols = pl.ds(c * CHUNK, CHUNK)
    copies = []
    for n, (ref, row) in enumerate(pieces):
        rows = ref.shape[0]
        copies.append(
            pltpu.make_async_copy(
                ref.at[:, cols], whole.at[pl.ds(pl.multiple_of(row, 64), rows), cols], sems.at[c, n]
            )
        )
    return copies


def grad_pieces(y, g, back, ahead, fa, fb):
    far = lax.rem(y + 2, 4) * TOK
    return [(g, y * TOK), (back, lax.rem(y + 3, 4) * TOK), (ahead, lax.rem(y + 1, 4) * TOK), (fa, far), (fb, far + 64)]


def block_kernel(at, *refs):
    g, (w, wa, wb, wc, wd, o), (mine, *other), hs = refs[:5], refs[5:11], refs[11:14], refs[14:18]
    gs, ws, term, staged, acc, gsem, wsem, osem = refs[18:]
    x, y, core = at[0], at[1], at[2]
    g_pieces = grad_pieces(y, *g)
    near = lax.select(core == 0, 1, 3)
    w_pieces = [
        (w, 0),
        (wa, near * TOK),
        (wb, (4 - near) * TOK),
        (wc, 2 * TOK + 64 * core),
        (wd, 2 * TOK + 64 * (1 - core)),
    ]
    g_copies = [chunk_copies(g_pieces, gs, gsem, c) for c in range(MODEL // CHUNK)]
    w_copies = [chunk_copies(w_pieces, ws, wsem, c) for c in range(MODEL // CHUNK)]
    for pair in zip(g_copies, w_copies):
        for copy in pair[0] + pair[1]:
            copy.start()
    outs = o[...].reshape(4 * TOK, 4 * HEAD)
    for c in range(MODEL // CHUNK):
        cols = pl.ds(c * CHUNK, CHUNK)
        for copy in g_copies[c]:
            copy.wait()
        term[cols, :] = tn(gs[:, cols], outs)
        for m in range(CHUNK * c // 200, CHUNK * (c + 1) // 200):
            staged[m] = term[pl.ds(200 * m, 200), :].astype(BF)
            z = m // 2
            inside = staged.at[m], mine.at[z], osem.at[m]
            outside = staged.at[m], other[z // 4].at[z % 4], osem.at[m]
            pl.when(core == m % 2)(lambda refs=inside: pltpu.make_async_copy(*refs).start())
            pl.when(core != m % 2)(lambda refs=outside: pltpu.make_async_copy(*refs).start())
        for copy in w_copies[c]:
            copy.wait()
        part = nt(gs[:, cols], ws[:, cols])
        if c == 0:
            acc[...] = part
        else:
            acc[...] += part
    for k in range(4):
        own = pl.ds(pl.multiple_of(lax.rem(x + 4 - k, 4) * HEAD, HEAD), HEAD)
        lines = []
        for j in range(4):
            rows = pl.ds(j * TOK, TOK)
            h = acc[rows, pl.ds(k * HEAD, HEAD)].astype(BF)
            hs[k][rows, :] = h
            product = h.astype(F32) * o[j, :, own].astype(F32)
            lines.append(jnp.sum(product.T, axis=0, keepdims=True))
        hs[k][pl.ds(4 * TOK, 16), :] = three_terms(jnp.concatenate(lines, axis=0))
    for m in range(16):
        pltpu.make_async_copy(staged.at[m], mine.at[m // 2], osem.at[m]).wait()


def blocks(at, g, w, o):
    vm = pl.BlockSpec(memory_space=pltpu.VMEM)
    sm = pl.BlockSpec(memory_space=pltpu.SMEM)
    hbm = pl.BlockSpec(memory_space=pl.ANY)
    sizes = [(n, 200, 4 * HEAD) for n in (8, 4, 4)] + [(4 * TOK + 16, HEAD)] * 4
    return pl.pallas_call(
        block_kernel,
        out_shape=[jax.ShapeDtypeStruct(size, BF) for size in sizes],
        in_specs=[sm] + [hbm] * 10 + [vm],
        out_specs=[hbm] * 3 + [vm] * 4,
        scratch_shapes=[
            pltpu.VMEM((4 * TOK, MODEL), BF),
            pltpu.VMEM((4 * HEAD, MODEL), BF),
            pltpu.VMEM((MODEL, 4 * HEAD), F32),
            pltpu.VMEM((16, 200, 4 * HEAD), BF),
            pltpu.VMEM((4 * TOK, 4 * HEAD), F32),
            pltpu.SemaphoreType.DMA((MODEL // CHUNK, 5)),
            pltpu.SemaphoreType.DMA((MODEL // CHUNK, 5)),
            pltpu.SemaphoreType.DMA((16,)),
        ],
        compiler_params=pltpu.CompilerParams(vmem_limit_bytes=60 * 1024 * 1024),
        cost_estimate=pl.CostEstimate(flops=10350000000, bytes_accessed=32400000, transcendentals=0),
        name="blocks",
    )(at, *g, *w, o)


def pair_kernel(at, mine, *refs):
    other, outs = refs[:2], refs[2:]
    for k in range(4):
        cols = pl.ds(pl.multiple_of(lax.rem(at[0] + k, 4) * HEAD, HEAD), HEAD)
        for z in range(8):
            outs[k][z] = (mine[z, :, cols].astype(F32) + other[z // 4][z % 4, :, cols].astype(F32)).astype(BF)


def pair_sum(at, mine, *other):
    vm = pl.BlockSpec(memory_space=pltpu.VMEM)
    sm = pl.BlockSpec(memory_space=pltpu.SMEM)
    return pl.pallas_call(
        pair_kernel,
        out_shape=[jax.ShapeDtypeStruct((8, 200, HEAD), BF)] * 4,
        in_specs=[sm] + [vm] * 3,
        out_specs=[vm] * 4,
        cost_estimate=pl.CostEstimate(flops=1, bytes_accessed=1, transcendentals=0),
        name="pair_sum",
    )(at, mine, *other)


def on_device(queries, keys_in, values_in, saved_out, out_grad, out_weight, image_units):
    seq = lax.axis_index("seq").astype(jnp.int32)
    dp = lax.axis_index("dp").astype(jnp.int32)
    core, z = lax.rem(dp, 2), lax.div(dp, 2)
    at = jnp.stack([lax.div(seq, 4), lax.rem(seq, 4), core, z])
    after = lax.optimization_barrier
    move = lax.ppermute

    g = out_grad[0]
    back, ahead = move(g, "seq", YS[1]), move(g, "seq", YS[3])
    wa = move(out_weight, ("dp", "seq"), BOTH)
    wc = move(lax.dynamic_slice_in_dim(out_weight, 64 * core, 64, 0), "seq", XS[2])
    o_rows = lax.all_to_all(
        pack_out(saved_out[0]), "seq", split_axis=0, concat_axis=0, tiled=True, axis_index_groups=YGROUPS
    )
    back, ahead, wa, wc, o_rows, at = after((back, ahead, wa, wc, o_rows, at))
    q, fa, fb = after((queries[0], back[:64], ahead[64:]))
    fa, fb = move(fa, "seq", YS[1]), move(fb, "seq", YS[3])
    wb, wd = move(wa, "dp", CORES), move(wc, "dp", CORES)
    qkv = lax.all_to_all(pack(q, keys_in[0], values_in[0]), "seq", split_axis=0, concat_axis=0, tiled=True)
    g_pieces = (g, back, ahead, fa, fb)

    mine, *other, h0, h1, h2, h3 = blocks(at, g_pieces, (out_weight, wa, wb, wc, wd), o_rows)
    heads = [h0] + [move(h, "seq", XS[4 - k]) for k, h in ((1, h1), (2, h2), (3, h3))]

    pairs = pair_sum(at, mine, *[move(part, "dp", CORES) for part in other])
    qkv, *_ = after((qkv, *pairs))
    grads = attention(at, image_units[0], qkv, heads)
    sent = lax.all_to_all(grads, "seq", split_axis=0, concat_axis=0, tiled=True)
    query_grad, key_grad, value_grad = unpack(sent)

    total = pairs[0].astype(F32)
    for k in (1, 2, 3):
        total = total + move(pairs[k], "seq", XS[k]).astype(F32)
    total = total.reshape(4, 2, 200, HEAD)
    bit, quarter = lax.rem(z, 2), lax.div(z, 2)
    away = lax.dynamic_index_in_dim(total, 1 - bit, 1, keepdims=False).astype(BF)
    total = lax.dynamic_index_in_dim(total, bit, 1, keepdims=False) + move(away, "dp", ZNEAR).astype(F32)
    parts = [lax.dynamic_index_in_dim(total, quarter, 0, keepdims=False)]
    for k in (1, 2, 3):
        part = lax.dynamic_index_in_dim(total, lax.rem(quarter + k, 4), 0, keepdims=False).astype(BF)
        parts.append(move(part, "dp", ZFAR[k]))
    *parts, query_grad, key_grad, value_grad = after((*parts, query_grad, key_grad, value_grad))
    last = sum([part.astype(F32) for part in parts[1:]], parts[0])
    weight_grad = last.T * (1.0 / math.sqrt(PACK * 16))
    return query_grad[None], key_grad[None], value_grad[None], weight_grad


def solution(mesh):
    rows = P("dp", "seq", None)
    return jax.shard_map(
        on_device,
        mesh=mesh,
        in_specs=(rows, rows, rows, rows, rows, P("seq", None), P("dp", None)),
        out_specs=(rows, rows, rows, P("seq", "dp")),
        check_vma=False,
    )
```
